32 devices in a mesh: fsdp: 8 (over z, core), tp: 4 (over y, x).
Axes of the slice: x: 2, y: 2, z: 4, core: 2. Of those that a mesh axis runs over, the one named last changes fastest.
Arguments:
- tokens: bfloat16 [6144, 4096], P('fsdp', 'tp'), may hold values from -14 to 14
- target: bfloat16 [6144, 4096], P('fsdp', 'tp'), may hold values from -6 to 6
- w_query: bfloat16 [4096, 4096], P('fsdp', 'tp'), may hold values from -0.09375 to 0.09375
- w_key: bfloat16 [4096, 1024], P('fsdp', 'tp'), may hold values from -0.09375 to 0.09375
- w_value: bfloat16 [4096, 1024], P('fsdp', 'tp'), may hold values from -0.09375 to 0.09375
- t_query: bfloat16 [4096, 4096], P('fsdp', 'tp'), may hold values from -0.09375 to 0.09375
- t_key: bfloat16 [4096, 1024], P('fsdp', 'tp'), may hold values from -0.09375 to 0.09375
- t_value: bfloat16 [4096, 1024], P('fsdp', 'tp'), may hold values from -0.09375 to 0.09375
Outputs:
- curve_query: float32 [4096, 4096], P('fsdp', 'tp')
- curve_key: float32 [4096, 1024], P('fsdp', 'tp')
- curve_value: float32 [4096, 1024], P('fsdp', 'tp')
The draws below stay inside these ranges and needn't reach their ends.
All inputs are finite; a program needn't handle non-finite values.
Results may differ from the reference program's by a relative error of at most 0.03.
The reference program's roundings to bfloat16 on the way count: a program that leaves them out, or rounds other values in their place, can miss the bound.
Values may be sent and summed in bfloat16 or wider, within the bound.
No kernel may reach another device: no remote copies, remote signals or barrier semaphores. Data moves between devices by JAX's collectives and lax.ppermute only.
A program may use at most 128 MiB of HBM per device.

```python
import math
import jax
import jax.numpy as jnp
from jax import lax

D = 4096
QH = 32
KVH = 8
HD = 128
TOK_DEV = 768
TOKENS = 6144


def draw_tokens(key, part):
    return jax.random.truncated_normal(key, -4.0, 4.0, (TOKENS, D), jnp.float32).astype(jnp.bfloat16)


def block_levels(stream_key, shape, shards, low, largest):
    def one(dim, parts):
        draws = jax.random.uniform(jax.random.fold_in(jax.random.fold_in(stream_key, 6), dim), (parts,), jnp.float32, low / len(shards), largest / len(shards))
        return jnp.repeat(jnp.exp(draws), shape[dim] // parts).reshape((-1,) + (1,) * (len(shape) - dim - 1))

    loudness = one(*shards[0])
    for cut in shards[1:]:
        loudness = loudness * one(*cut)
    return loudness


def noise(stream_key, dims, deviation, reach, shards=(), kind=jnp.bfloat16):
    factor_of = block_levels(stream_key, dims, shards, -0.22, 0.18) if shards else 1.0
    entries = jax.random.normal(stream_key, dims, jnp.float32) * deviation * factor_of
    return jnp.minimum(jnp.maximum(entries, -reach), reach).astype(kind)


def setup_inputs(seed: int = 0) -> dict:
    splits = jax.random.split(jax.random.key(seed), 9)
    return {
        "tokens": draw_tokens(jax.random.fold_in(splits[8], 71), 0),
        "target": noise(splits[1], (TOKENS, QH * HD), 1.0, 6.0, ((0, 8), (1, 4))),
        "w_query": noise(splits[2], (D, QH * HD), D ** -0.5, 0.09375, ((0, 8), (1, 4))),
        "w_key": noise(splits[3], (D, KVH * HD), D ** -0.5, 0.09375, ((0, 8), (1, 4))),
        "w_value": noise(splits[4], (D, KVH * HD), D ** -0.5, 0.09375, ((0, 8), (1, 4))),
        "t_query": noise(splits[5], (D, QH * HD), D ** -0.5, 0.09375, ((0, 8), (1, 4))),
        "t_key": noise(splits[6], (D, KVH * HD), D ** -0.5, 0.09375, ((0, 8), (1, 4))),
        "t_value": noise(splits[7], (D, KVH * HD), D ** -0.5, 0.09375, ((0, 8), (1, 4))),
    }


def rope_tables(length, width):
    halfway = width // 2
    frequency = jnp.exp(jnp.arange(halfway, dtype=jnp.float32) * (-2.0 * math.log(10000.0) / width))
    angles = jnp.arange(length, dtype=jnp.float32)[:, None] * frequency[None, :]
    return (jnp.cos(angles), jnp.sin(angles))

def rotate(inputs, cosine_table, sine_table):
    halfway = inputs.shape[1] // 2
    leading = inputs[:, :halfway]
    trailing = inputs[:, halfway:]
    return jnp.concatenate([leading * cosine_table - trailing * sine_table, trailing * cosine_table + leading * sine_table], axis=1)

def head_loss(query_head, key_head, value_head, target_head, cosine_table, sine_table, factor):
    length = query_head.shape[0]
    rotated_query = rotate(query_head, cosine_table, sine_table).astype(jnp.bfloat16)
    rotated_key = rotate(key_head, cosine_table, sine_table).astype(jnp.bfloat16)
    value_low = value_head.astype(jnp.bfloat16)
    scores = jnp.dot(rotated_query, rotated_key.T, preferred_element_type=jnp.float32) * query_head.shape[1] ** (-0.5)
    position = lax.broadcasted_iota(jnp.int32, (length, length), 0)
    earlier = lax.broadcasted_iota(jnp.int32, (length, length), 1)
    scores = jnp.where(earlier <= position, scores, -1e+30)
    weights = jax.nn.softmax(scores, axis=-1).astype(jnp.bfloat16)
    mixture = jnp.dot(weights, value_low, preferred_element_type=jnp.float32)
    mismatch = mixture - target_head.astype(jnp.float32)
    return 0.5 * factor * jnp.sum(mismatch * mismatch)

def group_curvature(query_group, key_group, value_group, tangent_query, tangent_key, tangent_value, target_group, cosine_table, sine_table, factor):

    def one_head(running, packed):
        query_head, tangent_head, target_head = packed

        def gradient(query_in, key_in, value_in):
            return jax.grad(head_loss, argnums=(0, 1, 2))(query_in, key_in, value_in, target_head, cosine_table, sine_table, factor)
        ignored, derived = jax.jvp(gradient, (query_head, key_group, value_group), (tangent_head, tangent_key, tangent_value))
        return ((running[0] + derived[1], running[1] + derived[2]), derived[0])
    blank_sum = jnp.zeros(key_group.shape, jnp.float32)
    packed_all = (jnp.moveaxis(query_group, 1, 0), jnp.moveaxis(tangent_query, 1, 0), jnp.moveaxis(target_group, 1, 0))
    totals, per_head = lax.scan(one_head, (blank_sum, blank_sum), packed_all)
    return (jnp.moveaxis(per_head, 0, 1), totals[0], totals[1])

def local_curvature(query, key_rows, value_rows, d_query, d_key, d_value, target_rows, factor, group_size, head_width):
    length = query.shape[0]
    cosine_table, sine_table = rope_tables(length, head_width)
    group_count = key_rows.shape[1] // head_width
    block_width = group_size * head_width
    query_parts, key_parts, value_parts = ([], [], [])
    for member in range(group_count):
        wide_lo = member * block_width
        wide_hi = wide_lo + block_width
        narrow_lo = member * head_width
        narrow_hi = narrow_lo + head_width
        dual_query, dual_key, dual_value = group_curvature(query[:, wide_lo:wide_hi].reshape(length, group_size, head_width), key_rows[:, narrow_lo:narrow_hi], value_rows[:, narrow_lo:narrow_hi], d_query[:, wide_lo:wide_hi].reshape(length, group_size, head_width), d_key[:, narrow_lo:narrow_hi], d_value[:, narrow_lo:narrow_hi], target_rows[:, wide_lo:wide_hi].reshape(length, group_size, head_width), cosine_table, sine_table, factor)
        query_parts.append(dual_query.reshape(length, block_width))
        key_parts.append(dual_key)
        value_parts.append(dual_value)
    low_query = jnp.concatenate(query_parts, axis=1).astype(jnp.bfloat16)
    low_key = jnp.concatenate(key_parts, axis=1).astype(jnp.bfloat16)
    low_value = jnp.concatenate(value_parts, axis=1).astype(jnp.bfloat16)
    return (low_query, low_key, low_value)

def rounded_part(sequence_rows, dual_low):
    term = lax.dot_general(sequence_rows, dual_low, (((0,), (0,)), ((), ())), preferred_element_type=jnp.float32)
    return lax.optimization_barrier(term.astype(jnp.bfloat16)).astype(jnp.float32)

def reference(tokens, target, w_query, w_key, w_value, t_query, t_key, t_value):
    factor = TOKENS ** (-0.5)

    def one_sequence(running, number):
        offset = number * TOK_DEV
        sequence_rows = lax.dynamic_slice_in_dim(tokens, offset, TOK_DEV, 0)
        wanted = lax.dynamic_slice_in_dim(target, offset, TOK_DEV, 0)
        projected = [jnp.dot(sequence_rows, weight, preferred_element_type=jnp.float32) for weight in (w_query, w_key, w_value, t_query, t_key, t_value)]
        cotangents = local_curvature(projected[0], projected[1], projected[2], projected[3], projected[4], projected[5], wanted, factor, QH // KVH, HD)
        updated = tuple((total_in + rounded_part(sequence_rows, dual_low) for total_in, dual_low in zip(running, cotangents)))
        return (updated, None)
    initial = (jnp.zeros((D, QH * HD), jnp.float32), jnp.zeros((D, KVH * HD), jnp.float32), jnp.zeros((D, KVH * HD), jnp.float32))
    result, ignored = lax.scan(one_sequence, initial, jnp.arange(TOKENS // TOK_DEV, dtype=jnp.int32))
    return (result[0], result[1], result[2])
```

```python
import functools
import math

import jax
import jax.numpy as jnp
from jax import lax
from jax.experimental import pallas as pl
from jax.experimental.pallas import tpu as pltpu
from jax.sharding import PartitionSpec as P

HD = 128
SMALL = pl.CostEstimate(flops=1000, bytes_accessed=1000, transcendentals=0)
SIDE = 512
ROWS = 256


def rope_tables(length, width):
    halfway = width // 2
    frequency = jnp.exp(jnp.arange(halfway, dtype=jnp.float32) * (-2.0 * math.log(10000.0) / width))
    angles = jnp.arange(length, dtype=jnp.float32)[:, None] * frequency[None, :]
    cosine, sine = jnp.cos(angles), jnp.sin(angles)
    return jnp.concatenate([cosine, cosine], axis=1), jnp.concatenate([-sine, sine], axis=1)


def mm(a, b):
    return jnp.dot(a, b, preferred_element_type=jnp.float32)


def mm_nt(a, b):
    return lax.dot_general(a, b, (((1,), (1,)), ((), ())), preferred_element_type=jnp.float32)


def slab_copies(places, features, slabs, x_buf, w_buf, sems):
    depth = slabs[0].shape[-2]
    copies = []
    for n, slab in enumerate(slabs):
        here = pl.ds(n * depth, depth)
        column = pl.ds(pl.multiple_of(places[n + 1] * depth, depth), depth)
        copies.append(pltpu.make_async_copy(slab, w_buf.at[here, :], sems.at[2 * n]))
        copies.append(
            pltpu.make_async_copy(features.at[:, column], x_buf.at[:, here], sems.at[2 * n + 1])
        )
    return copies


def project(copies, x_buf, w_buf, out, early):
    depth, width = w_buf.shape
    slabs = len(copies) // 2
    cuts = [0, slabs] if slabs == 2 else [0, 2, slabs]
    for copy in copies[:2 * cuts[1]]:
        copy.start()
    for n in range(len(cuts) - 1):
        for copy in copies[2 * cuts[n]:2 * cuts[n + 1]]:
            copy.wait()
        if n + 2 < len(cuts):
            for copy in copies[2 * cuts[n + 1]:]:
                copy.start()
        ks = slice(cuts[n] * depth // slabs, cuts[n + 1] * depth // slabs)
        for left in range(0, width, SIDE):
            columns = pl.ds(left, SIDE)
            total = mm(x_buf[:, ks], w_buf[ks, columns])
            if n:
                total += out[:, columns]
            elif early is not None:
                total += early[:, columns]
            out[:, columns] = total


def fold_kernel(pairs, places, *refs):
    x_buf, w_buf, sems = refs[pairs + 2:]

    @pl.when(places[0] == 1)
    def _():
        copies = slab_copies(places, refs[0], refs[1:pairs + 1], x_buf, w_buf, sems)
        project(copies, x_buf, w_buf, refs[pairs + 1], None)


def fold(features, slabs, places):
    rows = features.shape[0]
    depth, width = slabs[0].shape
    pairs = len(slabs)
    slow = pl.BlockSpec(memory_space=pltpu.HBM)
    return pl.pallas_call(
        functools.partial(fold_kernel, pairs),
        grid_spec=pltpu.PrefetchScalarGridSpec(
            num_scalar_prefetch=1,
            grid=(),
            in_specs=[slow] * (pairs + 1),
            out_specs=pl.BlockSpec((rows, width), lambda p: (0, 0)),
            scratch_shapes=[
                pltpu.VMEM((rows, pairs * depth), jnp.bfloat16),
                pltpu.VMEM((pairs * depth, width), jnp.bfloat16),
                pltpu.SemaphoreType.DMA((2 * pairs,)),
            ],
        ),
        out_shape=jax.ShapeDtypeStruct((rows, width), jnp.float32),
        compiler_params=pltpu.CompilerParams(vmem_limit_bytes=48 * 2 ** 20),
        cost_estimate=SMALL,
        name="fold_projections",
    )(places, features, *slabs)


def place_kernel(places, *refs):
    pieces, (out, mine, theirs) = refs[:-3], refs[-3:]
    for n, ref in enumerate(pieces):

        @pl.when(pl.program_id(0) // 2 == n)
        def _():
            out[...] = ref[0]
            turned = ref[0].T
            mine[...] = turned
            theirs[...] = turned


def place(stacks, columns, core):
    rows, width = stacks[0].shape[1:]
    count = 2 * len(stacks)
    half = [n // 2 % 2 for n in range(count)]
    spare = len(stacks)
    tables = [
        [2 * columns[n] + half[n] for n in range(count)],
        [jnp.where(core == half[n], columns[n], spare) for n in range(count)],
        [jnp.where(core == half[n], spare, columns[n]) for n in range(count)],
    ]
    tables = jnp.stack([jnp.stack(table) for table in tables]).astype(jnp.int32)

    def piece(n):
        return pl.BlockSpec((1, rows, width), lambda i, p: (jnp.clip(i - 2 * n, 0, 1), 0, 0))

    return pl.pallas_call(
        place_kernel,
        grid_spec=pltpu.PrefetchScalarGridSpec(
            num_scalar_prefetch=1,
            grid=(count,),
            in_specs=[piece(n) for n in range(len(stacks))],
            out_specs=[
                pl.BlockSpec((rows, width), lambda i, p: (0, p[0, i])),
                pl.BlockSpec((width, rows), lambda i, p: (p[1, i], 0)),
                pl.BlockSpec((width, rows), lambda i, p: (p[2, i], 0)),
            ],
        ),
        out_shape=[jax.ShapeDtypeStruct((rows, count * width), stacks[0].dtype)]
        + [jax.ShapeDtypeStruct(((spare + 1) * width, rows), stacks[0].dtype)] * 2,
        compiler_params=pltpu.CompilerParams(
            dimension_semantics=("arbitrary",), vmem_limit_bytes=32 * 2 ** 20
        ),
        cost_estimate=SMALL,
        name="place_tokens",
    )(tables, *stacks)


def gradient_kernel(pairs, outs, _, *refs):
    total = None
    for n in range(pairs):
        term = mm(refs[n][...], refs[pairs + n][...])
        total = term if total is None else total + term
    each = pl.num_programs(0) // outs
    for n in range(outs):

        @pl.when(pl.program_id(0) // each == n)
        def _():
            refs[2 * pairs + n][0] = total.astype(jnp.bfloat16)


def gradient(features, lows, blocks, outs=1):
    length, width = lows[0].shape
    depth = features[0].shape[0] // 5
    pairs, count = len(features), blocks.shape[0]
    each = count // outs

    def part(n):
        return pl.BlockSpec(
            (1, depth, width), lambda i, p: (jnp.clip(i - n * each, 0, each - 1), 0, 0)
        )

    return pl.pallas_call(
        functools.partial(gradient_kernel, pairs, outs),
        grid_spec=pltpu.PrefetchScalarGridSpec(
            num_scalar_prefetch=1,
            grid=(count,),
            in_specs=[pl.BlockSpec((depth, length), lambda i, p: (p[i], 0))] * pairs
            + [pl.BlockSpec((length, width), lambda i, p: (0, 0))] * pairs,
            out_specs=[part(n) for n in range(outs)],
        ),
        out_shape=[jax.ShapeDtypeStruct((each, depth, width), jnp.bfloat16)] * outs,
        compiler_params=pltpu.CompilerParams(
            dimension_semantics=("arbitrary",), vmem_limit_bytes=48 * 2 ** 20
        ),
        cost_estimate=SMALL,
        name="gradient_rows",
    )(blocks, *features, *lows)


def attention_kernel(members, factor, late, has_early, places, *refs):
    features, refs = (refs[0], refs[1:]) if late else (None, refs)
    slabs, refs = refs[:late], refs[late:]
    early_ref, refs = (refs[0], refs[1:]) if has_early else (None, refs)
    wanted_ref, cos_ref, sin_ref, low_ref, kcat, vcat, qcat, dkt, dvt = refs[:9]
    proj, x_buf, w_buf, sems = refs[9:] if late else (early_ref, None, None, None)
    head = pl.program_id(0)
    length = cos_ref.shape[0]
    wide = members * HD
    half = wide + 2 * HD
    scale = HD ** -0.5
    bf16, f32 = jnp.bfloat16, jnp.float32

    def rope(u):
        return u * cos_ref[...] + pltpu.roll(u, HD // 2, 1) * sin_ref[...]

    def unrope(u, rows):
        return u * cos_ref[rows, :] - pltpu.roll(u, HD // 2, 1) * sin_ref[rows, :]

    active = places[0] == 1

    @pl.when((head == 0) & (places[0] == 0))
    def _():
        low_ref[...] = jnp.zeros_like(low_ref)

    @pl.when((head == 0) & active)
    def _():
        if late:
            copies = slab_copies(places, features, slabs, x_buf, w_buf, sems)
            project(copies, x_buf, w_buf, proj, early_ref)
        kcat[:, :HD] = rope(proj[:, wide:wide + HD]).astype(bf16)
        kcat[:, HD:] = rope(proj[:, half + wide:half + wide + HD]).astype(bf16)
        vcat[:, :HD] = proj[:, wide + HD:half].astype(bf16)
        vcat[:, HD:] = proj[:, half + wide + HD:].astype(bf16)
        dkt[...] = jnp.zeros_like(dkt)
        dvt[...] = jnp.zeros_like(dvt)

    @pl.when(active)
    def _():
        qcat[:, :HD] = rope(proj[:, pl.ds(pl.multiple_of(half + head * HD, HD), HD)]).astype(bf16)
        qcat[:, HD:] = rope(proj[:, pl.ds(pl.multiple_of(head * HD, HD), HD)]).astype(bf16)

        for block in range(length // ROWS):
            rows = pl.ds(block * ROWS, ROWS)
            span = (block + 1) * ROWS
            keys, values = kcat[:span, :], vcat[:span, :]
            both = qcat[rows, :]
            scores = mm_nt(both[:, HD:], keys[:, :HD]) * scale
            position = lax.broadcasted_iota(jnp.int32, (ROWS, span), 0) + block * ROWS
            earlier = lax.broadcasted_iota(jnp.int32, (ROWS, span), 1)
            scores = jnp.where(earlier <= position, scores, -1e30)
            top = jnp.max(scores, axis=1, keepdims=True)
            grown = jnp.exp(scores - top)
            weights = grown * (1.0 / jnp.sum(grown, axis=1, keepdims=True))
            low_weights = weights.astype(bf16)
            d_scores = mm_nt(both, keys)
            d_scores = d_scores - jnp.sum(weights * d_scores, axis=1, keepdims=True)
            d_weights = weights * d_scores
            low_d_weights = d_weights.astype(bf16)
            mixed = mm(low_weights, values)
            mixture = mixed[:, :HD]
            miss = (mixture - wanted_ref[rows, :].astype(f32)).astype(bf16)
            d_miss = (mixed[:, HD:] + mm(low_d_weights, values[:, :HD]) * scale).astype(bf16)
            miss32, d_miss32 = miss.astype(f32), d_miss.astype(f32)
            mean = jnp.sum(miss32 * mixture, axis=1, keepdims=True)
            d_mean = jnp.sum(d_miss32 * mixture + miss32 * d_miss32, axis=1, keepdims=True)
            away = mm_nt(miss, values[:, :HD]) - mean
            d_away = mm_nt(jnp.concatenate([d_miss, miss], axis=1), values) - d_mean
            back = (weights * away).astype(bf16)
            d_back = (weights * (scale * (d_scores * away) + d_away)).astype(bf16)
            dual_q = mm(d_back, keys[:, :HD]) + mm(back, keys[:, HD:])
            low_ref[rows, pl.ds(pl.multiple_of(head * HD, HD), HD)] = unrope(
                dual_q * (scale * factor), rows
            ).astype(bf16)
            stacked = jnp.concatenate([both[:, HD:], both[:, :HD]], axis=0).T
            dkt[:, :span] += mm(stacked, jnp.concatenate([d_back, back], axis=0))
            stacked = jnp.concatenate([(miss32 * scale).astype(bf16), d_miss], axis=0).T
            dvt[:, :span] += mm(stacked, jnp.concatenate([low_d_weights, low_weights], axis=0))

    @pl.when((head == members - 1) & active)
    def _():
        every = pl.ds(0, length)
        low_ref[:, wide:wide + HD] = unrope(dkt[...].T * (scale * factor), every).astype(bf16)
        low_ref[:, wide + HD:] = (dvt[...].T * factor).astype(bf16)


def attention(wanted, first, width, tables, factor, early=None, features=None, slabs=(), places=None):
    length = wanted.shape[0]
    half = width // 2
    members = half // HD - 2
    first = first // HD
    late = len(slabs)
    if places is None:
        places = jnp.ones((1,), jnp.int32)
    slow = pl.BlockSpec(memory_space=pltpu.HBM)
    table = pl.BlockSpec((length, HD), lambda h, p: (0, 0))
    early_spec = [pl.BlockSpec((length, width), lambda h, p: (0, 0))]
    scratch = [pltpu.VMEM((length, 2 * HD), jnp.bfloat16)] * 3
    scratch += [pltpu.VMEM((HD, length), jnp.float32)] * 2
    if late:
        depth = late * slabs[0].shape[0]
        scratch += [
            pltpu.VMEM((length, width), jnp.float32),
            pltpu.VMEM((length, depth), jnp.bfloat16),
            pltpu.VMEM((depth, width), jnp.bfloat16),
            pltpu.SemaphoreType.DMA((2 * late,)),
        ]
    return pl.pallas_call(
        functools.partial(attention_kernel, members, factor, late, early is not None),
        grid_spec=pltpu.PrefetchScalarGridSpec(
            num_scalar_prefetch=1,
            grid=(members,),
            in_specs=[slow] * (late + 1 if late else 0)
            + (early_spec if early is not None else [])
            + [pl.BlockSpec((length, HD), lambda h, p: (0, first + h)), table, table],
            out_specs=pl.BlockSpec((length, half), lambda h, p: (0, 0)),
            scratch_shapes=scratch,
        ),
        out_shape=jax.ShapeDtypeStruct((length, half), jnp.bfloat16),
        compiler_params=pltpu.CompilerParams(
            dimension_semantics=("arbitrary",), vmem_limit_bytes=56 * 2 ** 20
        ),
        cost_estimate=SMALL,
        name="attention_curvature",
    )(places, *((features, *slabs) if late else ()), *(() if early is None else (early,)), wanted, *tables)


def pack_kernel(*refs):
    groups = refs[1].shape[1] // HD
    for g in range(groups):
        left = 0
        for ref in refs[:-groups]:
            width = ref.shape[1] // groups
            refs[g - groups][:, left:left + width] = ref[:, g * width:(g + 1) * width]
            left += width


def packed(parts):
    rows = parts[0].shape[0]
    groups = parts[1].shape[1] // HD
    width = sum(part.shape[1] for part in parts) // groups
    steps = 2
    return pl.pallas_call(
        pack_kernel,
        grid=(steps,),
        in_specs=[pl.BlockSpec((rows // steps, part.shape[1]), lambda i: (i, 0)) for part in parts],
        out_specs=[pl.BlockSpec((rows // steps, width), lambda i: (i, 0))] * groups,
        out_shape=[jax.ShapeDtypeStruct((rows, width), parts[0].dtype)] * groups,
        cost_estimate=SMALL,
        name="pack_rows",
    )(*parts)


def finish_kernel(inner, total_a, home, crossed, back, out_q, out_k, out_v):
    f32 = jnp.float32
    mine = inner[0] == 1
    total_b = jnp.where(
        mine, home[...].astype(f32) + crossed[...].astype(f32), back[...].astype(f32)
    )
    wide = total_b.shape[1] - 2 * HD
    for n, total in enumerate((total_a[...], total_b)):
        out_q[:, n * wide:(n + 1) * wide] = total[:, :wide]
        out_k[:, n * HD:(n + 1) * HD] = total[:, wide:wide + HD]
        out_v[:, n * HD:(n + 1) * HD] = total[:, wide + HD:]


def finish(inner, *terms):
    rows, width = terms[0].shape
    widths = (2 * (width - 2 * HD), 2 * HD, 2 * HD)
    block = rows // 2
    return pl.pallas_call(
        finish_kernel,
        grid_spec=pltpu.PrefetchScalarGridSpec(
            num_scalar_prefetch=1,
            grid=(2,),
            in_specs=[pl.BlockSpec((block, width), lambda i, p: (i, 0))] * len(terms),
            out_specs=[pl.BlockSpec((block, w), lambda i, p: (i, 0)) for w in widths],
        ),
        out_shape=[jax.ShapeDtypeStruct((rows, w), jnp.float32) for w in widths],
        cost_estimate=SMALL,
        name="finish_sums",
    )(inner.astype(jnp.int32)[None], *terms)


def unpacked(sums):
    wide = sums[0].shape[1] - 2 * HD
    return tuple(
        jnp.concatenate([s[:, lo:hi] for s in sums], axis=1)
        for lo, hi in ((0, wide), (wide, wide + HD), (wide + HD, wide + 2 * HD))
    )


def transposed_product(features, low):
    return lax.dot_general(
        features, low, (((0,), (0,)), ((), ())), preferred_element_type=jnp.float32
    ).astype(jnp.bfloat16)


def by_sequence(tokens, target, *parts):
    length = tokens.shape[0]
    factor = (length * lax.axis_size("fsdp")) ** (-0.5)
    groups = parts[1].shape[1] // HD
    wide = target.shape[1] // groups
    features = lax.all_gather(tokens, "tp", axis=1, tiled=True)
    gathered = [lax.all_gather(rows, "fsdp", axis=0, tiled=True) for rows in packed(parts)]
    tables = rope_tables(length, HD)
    sums = []
    for g in range(groups):
        early = mm(features, gathered[g])
        low = attention(target, g * wide, early.shape[1], tables, factor, early)
        part = transposed_product(features, low)
        sums.append(lax.psum_scatter(part, "fsdp", scatter_dimension=0, tiled=True).astype(jnp.float32))
    return unpacked(sums)


def after(value, *others):
    return lax.optimization_barrier((value,) + others)[0]


def inner_heavy(tokens, target, *parts):
    f32, bf16 = jnp.float32, jnp.bfloat16
    length = tokens.shape[0]
    position = lax.axis_index("fsdp")
    chip, core = position // 2, position % 2
    side, low_high = chip // 2, chip % 2
    inner = (chip == 1) | (chip == 2)
    factor = (length * lax.axis_size("fsdp")) ** (-0.5)
    wide = target.shape[1] // 2

    def chips(pairs):
        return [(2 * a + c, 2 * b + c) for a, b in pairs for c in range(2)]

    swap_sides = chips([(0, 1), (1, 0), (2, 3), (3, 2)])
    inwards, outwards = chips([(0, 1), (3, 2)]), chips([(1, 0), (2, 3)])
    middle, beyond = chips([(1, 2), (2, 1)]), chips([(0, 2), (3, 1)])
    swap_cores = [(n, n ^ 1) for n in range(8)]

    def along(value, pairs):
        return lax.ppermute(value, "fsdp", pairs)

    def other_core(value):
        return along(value, swap_cores)

    def across(value, bit):
        return lax.ppermute(value, "tp", [(n, n ^ bit) for n in range(4)])

    def halves(rows):
        return rows[:, :rows.shape[1] // 2], rows[:, rows.shape[1] // 2:]

    column = lax.axis_index("tp")
    columns = [column ^ bit for bit in (0, 1, 0, 2, 2, 3, 1, 3)]
    oi, oo = jnp.where(side == 0, 2, 1), jnp.where(side == 0, 3, 0)
    hi, ho = 3 - oi, 3 - oo
    slots = [2 * z + c for z in (chip, chip ^ 1, oi, oo) for c in (core, 1 - core)]

    def places(active, which=range(8)):
        return jnp.stack([active] + [slots[n] for n in which]).astype(jnp.int32)

    def plus(*terms):
        return functools.reduce(jnp.add, [term.astype(f32) for term in terms])

    tables = rope_tables(length, HD)

    phase = lax.optimization_barrier
    own_a, own_b = packed(parts)
    width = own_a.shape[1]
    first, second = halves(tokens)
    x_first, y_second = across(first, 1), across(second, 2)
    side_a, mid_a, own_a2 = phase(
        (along(own_a, swap_sides), along(own_a, middle), other_core(own_a))
    )
    outer_tokens = along(after(jnp.stack([first, second]), side_a), inwards)
    firsts, seconds = jnp.stack([first, x_first]), jnp.stack([second, y_second])
    pieces = [firsts, seconds, across(firsts, 2), across(seconds, 1)]
    features, mine_t, theirs_t = place(pieces, columns, core)
    late_side, late_mid = phase((side_a, mid_a, features))[:2]
    far_a, out_a, outer_tokens, side_a2, mid_a2, features = phase(
        (
            along(side_a, middle), along(mid_a, outwards), outer_tokens,
            other_core(late_side), other_core(late_mid), features,
        )
    )
    far_a2, out_a2, own_b = other_core(far_a), other_core(out_a), after(own_b, far_a)
    first, second = phase((outer_tokens[0], outer_tokens[1], far_a2, out_a2))[:2]
    slabs_a = [own_a, own_a2, side_a, side_a2, mid_a, mid_a2, far_a, far_a2]
    inner_low = attention(target, 0, width, tables, factor, None, features, slabs_a, places(inner))
    early = fold(
        features, [own_a, own_a2, side_a, side_a2, out_a, out_a2], places(~inner, range(6))
    )
    x_first, y_second, out_far_a, mid_b, side_b, inner_low, early = phase(
        (
            across(first, 1), across(second, 2), along(far_a, outwards), along(own_b, middle),
            along(own_b, inwards), inner_low, early,
        )
    )
    far_b, own_b = along(side_b, middle), after(own_b, inner_low)
    out_far_a2, mid_b2, side_b2, own_b2 = phase(
        tuple(other_core(rows) for rows in (out_far_a, mid_b, side_b, own_b))
    )
    outer_wanted = along(after(target[:, wide:], out_far_a2), inwards)
    firsts, seconds = jnp.stack([first, x_first]), jnp.stack([second, y_second])
    outer_low = attention(
        target, 0, width, tables, factor, early, features, [out_far_a, out_far_a2],
        places(~inner, (6, 7)),
    )
    low_a = jnp.where(inner, inner_low, outer_low)
    slabs_b = [own_b, own_b2, side_b, side_b2, mid_b, mid_b2]
    early = fold(features, slabs_b, places(inner, range(6)))
    far_b, early, low_a, firsts, seconds, theirs_t, outer_wanted = phase(
        (far_b, early, low_a, firsts, seconds, theirs_t, outer_wanted)
    )

    far_b2 = other_core(far_b)
    rows_t, lows = [mine_t, other_core(theirs_t)], [low_a, other_core(low_a)]
    away, home = gradient(rows_t, lows, jnp.stack([oo, oi, ho, hi]), 2)
    from_outer = along(away, inwards)
    pieces = [firsts, seconds, across(firsts, 2), across(seconds, 1)]
    own_low = attention(
        target, wide, width, tables, factor, early, features, [far_b, far_b2],
        places(inner, (6, 7)),
    )
    pieces[0] = after(pieces[0], own_low)
    outer_features, mine_t, theirs_t = place(pieces, columns, core)
    from_outer, own_low, outer_features, theirs_t = phase(
        (from_outer, own_low, outer_features, theirs_t)
    )
    crossed = along(plus(away, from_outer).astype(bf16), middle)
    own_low2, theirs_t = other_core(own_low), other_core(theirs_t)
    to_inner = along(after(home[1], from_outer), inwards)
    outer_low = attention(
        outer_wanted, 0, width, tables, factor, None, outer_features,
        slabs_b + [far_b, far_b2], places(inner),
    )
    rows_t += [mine_t, theirs_t]
    lows = [own_low, own_low2, outer_low, other_core(outer_low)]
    ready = phase((jnp.stack([oo, oi, ho, hi]), crossed, theirs_t, own_low2))[0]
    away_out = gradient(rows_t, lows, ready[:1])[0]
    away_in = gradient(rows_t, lows, after(ready[1:2], away_out))[0]
    crossed_out, crossed_in = along(away_out[0], middle), along(away_in[0], middle)
    back_a = along(plus(home[0], crossed[0]).astype(bf16), outwards)
    total_a = jnp.where(inner, home[1], home[0]).astype(f32) + plus(to_inner, crossed[1], back_a)
    home = gradient(rows_t, lows, after(ready[2:], away_in))[0]
    back_b = along(plus(home[0], crossed_out).astype(bf16), outwards)
    return finish(inner, total_a, home[1], crossed_in, back_b)


def solution(mesh):
    spec = P("fsdp", "tp")

    def shards(*args):
        groups = args[3].shape[1] // HD
        if mesh.shape["fsdp"] == 8 and mesh.shape["tp"] == 4 and groups == 2:
            return tuple(inner_heavy(*args))
        return by_sequence(*args)

    return jax.shard_map(
        shards,
        mesh=mesh,
        in_specs=(spec,) * 8,
        out_specs=(spec,) * 3,
        check_vma=False,
    )
```

```python
import functools
import math

import jax
import jax.numpy as jnp
from jax import lax
from jax.experimental import pallas as pl
from jax.experimental.pallas import tpu as pltpu
from jax.sharding import PartitionSpec as P

HD = 128
SMALL = pl.CostEstimate(flops=1000, bytes_accessed=1000, transcendentals=0)
SIDE = 512
ROWS = 256


def rope_tables(length, width):
    halfway = width // 2
    frequency = jnp.exp(jnp.arange(halfway, dtype=jnp.float32) * (-2.0 * math.log(10000.0) / width))
    angles = jnp.arange(length, dtype=jnp.float32)[:, None] * frequency[None, :]
    cosine, sine = jnp.cos(angles), jnp.sin(angles)
    return jnp.concatenate([cosine, cosine], axis=1), jnp.concatenate([-sine, sine], axis=1)


def mm(a, b):
    return jnp.dot(a, b, preferred_element_type=jnp.float32)


def mm_nt(a, b):
    return lax.dot_general(a, b, (((1,), (1,)), ((), ())), preferred_element_type=jnp.float32)


def slab_copies(places, features, slabs, x_buf, w_buf, sems):
    depth = slabs[0].shape[-2]
    copies = []
    for n, slab in enumerate(slabs):
        here = pl.ds(n * depth, depth)
        column = pl.ds(pl.multiple_of(places[n + 1] * depth, depth), depth)
        copies.append(pltpu.make_async_copy(slab, w_buf.at[here, :], sems.at[2 * n]))
        copies.append(
            pltpu.make_async_copy(features.at[:, column], x_buf.at[:, here], sems.at[2 * n + 1])
        )
    return copies


def project(copies, x_buf, w_buf, out, add):
    depth, width = w_buf.shape
    slabs = len(copies) // 2
    cuts = [0, slabs] if slabs == 2 else [0, 2, slabs]
    for copy in copies[:2 * cuts[1]]:
        copy.start()
    for n in range(len(cuts) - 1):
        for copy in copies[2 * cuts[n]:2 * cuts[n + 1]]:
            copy.wait()
        if n + 2 < len(cuts):
            for copy in copies[2 * cuts[n + 1]:]:
                copy.start()
        ks = slice(cuts[n] * depth // slabs, cuts[n + 1] * depth // slabs)
        for left in range(0, width, SIDE):
            columns = pl.ds(left, SIDE)
            total = mm(x_buf[:, ks], w_buf[ks, columns])
            if n or add:
                total += out[:, columns]
            out[:, columns] = total


def fold_kernel(pairs, places, *refs):
    x_buf, w_buf, sems = refs[pairs + 2:]

    @pl.when(places[0] == 1)
    def _():
        copies = slab_copies(places, refs[0], refs[1:pairs + 1], x_buf, w_buf, sems)
        project(copies, x_buf, w_buf, refs[pairs + 1], False)


def fold(features, slabs, places):
    rows = features.shape[0]
    depth, width = slabs[0].shape
    pairs = len(slabs)
    slow = pl.BlockSpec(memory_space=pltpu.HBM)
    return pl.pallas_call(
        functools.partial(fold_kernel, pairs),
        grid_spec=pltpu.PrefetchScalarGridSpec(
            num_scalar_prefetch=1,
            grid=(),
            in_specs=[slow] * (pairs + 1),
            out_specs=pl.BlockSpec((rows, width), lambda p: (0, 0)),
            scratch_shapes=[
                pltpu.VMEM((rows, pairs * depth), jnp.bfloat16),
                pltpu.VMEM((pairs * depth, width), jnp.bfloat16),
                pltpu.SemaphoreType.DMA((2 * pairs,)),
            ],
        ),
        out_shape=jax.ShapeDtypeStruct((rows, width), jnp.float32),
        compiler_params=pltpu.CompilerParams(vmem_limit_bytes=48 * 2 ** 20),
        cost_estimate=SMALL,
        name="fold_projections",
    )(places, features, *slabs)


def place_kernel(places, *refs):
    pieces, (out, mine, theirs) = refs[:-3], refs[-3:]
    for n, ref in enumerate(pieces):

        @pl.when(pl.program_id(0) // 2 == n)
        def _():
            out[...] = ref[0]
            turned = ref[0].T
            mine[...] = turned
            theirs[...] = turned


def place(stacks, columns, core):
    rows, width = stacks[0].shape[1:]
    count = 2 * len(stacks)
    half = [n // 2 % 2 for n in range(count)]
    spare = len(stacks)
    tables = [
        [2 * columns[n] + half[n] for n in range(count)],
        [jnp.where(core == half[n], columns[n], spare) for n in range(count)],
        [jnp.where(core == half[n], spare, columns[n]) for n in range(count)],
    ]
    tables = jnp.stack([jnp.stack(table) for table in tables]).astype(jnp.int32)

    def piece(n):
        return pl.BlockSpec((1, rows, width), lambda i, p: (jnp.clip(i - 2 * n, 0, 1), 0, 0))

    return pl.pallas_call(
        place_kernel,
        grid_spec=pltpu.PrefetchScalarGridSpec(
            num_scalar_prefetch=1,
            grid=(count,),
            in_specs=[piece(n) for n in range(len(stacks))],
            out_specs=[
                pl.BlockSpec((rows, width), lambda i, p: (0, p[0, i])),
                pl.BlockSpec((width, rows), lambda i, p: (p[1, i], 0)),
                pl.BlockSpec((width, rows), lambda i, p: (p[2, i], 0)),
            ],
        ),
        out_shape=[pltpu.HBM((rows, count * width), stacks[0].dtype)]
        + [pltpu.HBM(((spare + 1) * width, rows), stacks[0].dtype)] * 2,
        compiler_params=pltpu.CompilerParams(
            dimension_semantics=("arbitrary",), vmem_limit_bytes=32 * 2 ** 20
        ),
        cost_estimate=SMALL,
        name="place_tokens",
    )(tables, *stacks)


def gradient_kernel(pairs, outs, _, *refs):
    total = None
    for n in range(pairs):
        term = mm(refs[n][...], refs[pairs + n][...])
        total = term if total is None else total + term
    each = pl.num_programs(0) // outs
    for n in range(outs):

        @pl.when(pl.program_id(0) // each == n)
        def _():
            refs[2 * pairs + n][0] = total.astype(jnp.bfloat16)


def gradient(features, lows, blocks, outs=1):
    length, width = lows[0].shape
    depth = features[0].shape[0] // 5
    pairs, count = len(features), blocks.shape[0]
    each = count // outs

    def part(n):
        return pl.BlockSpec(
            (1, depth, width), lambda i, p: (jnp.clip(i - n * each, 0, each - 1), 0, 0)
        )

    return pl.pallas_call(
        functools.partial(gradient_kernel, pairs, outs),
        grid_spec=pltpu.PrefetchScalarGridSpec(
            num_scalar_prefetch=1,
            grid=(count,),
            in_specs=[pl.BlockSpec((depth, length), lambda i, p: (p[i], 0))] * pairs
            + [pl.BlockSpec((length, width), lambda i, p: (0, 0))] * pairs,
            out_specs=[part(n) for n in range(outs)],
        ),
        out_shape=[jax.ShapeDtypeStruct((each, depth, width), jnp.bfloat16)] * outs,
        compiler_params=pltpu.CompilerParams(
            dimension_semantics=("arbitrary",), vmem_limit_bytes=48 * 2 ** 20
        ),
        cost_estimate=SMALL,
        name="gradient_rows",
    )(blocks, *features, *lows)


def attention_kernel(members, factor, late, has_early, places, *refs):
    features, refs = (refs[0], refs[1:]) if late else (None, refs)
    slabs, refs = refs[:late], refs[late:]
    early_ref, refs = (refs[0], refs[1:]) if has_early else (None, refs)
    wanted_ref, cos_ref, sin_ref, low_ref, kcat, vcat, qcat, dkt, dvt = refs[:9]
    proj, x_buf, w_buf, sems = refs[9:] if late else (early_ref, None, None, None)
    head = pl.program_id(0)
    length = cos_ref.shape[0]
    wide = members * HD
    half = wide + 2 * HD
    scale = HD ** -0.5
    bf16, f32 = jnp.bfloat16, jnp.float32

    def rope(u):
        return u * cos_ref[...] + pltpu.roll(u, HD // 2, 1) * sin_ref[...]

    def unrope(u, rows):
        return u * cos_ref[rows, :] - pltpu.roll(u, HD // 2, 1) * sin_ref[rows, :]

    active = places[0] == 1

    @pl.when((head == 0) & (places[0] == 0))
    def _():
        low_ref[...] = jnp.zeros_like(low_ref)

    @pl.when((head == 0) & active)
    def _():
        if late:
            copies = slab_copies(places, features, slabs, x_buf, w_buf, sems)
            if has_early:
                fetched = pltpu.make_async_copy(early_ref, proj, sems.at[2 * late])
                fetched.start()
                fetched.wait()
            project(copies, x_buf, w_buf, proj, has_early)
        kcat[:, :HD] = rope(proj[:, wide:wide + HD]).astype(bf16)
        kcat[:, HD:] = rope(proj[:, half + wide:half + wide + HD]).astype(bf16)
        vcat[:, :HD] = proj[:, wide + HD:half].astype(bf16)
        vcat[:, HD:] = proj[:, half + wide + HD:].astype(bf16)
        dkt[...] = jnp.zeros_like(dkt)
        dvt[...] = jnp.zeros_like(dvt)

    @pl.when(active)
    def _():
        pair = range(2)
        for n in pair:
            left = pl.multiple_of((2 * head + n) * HD, HD)
            qcat[n, :, :HD] = rope(proj[:, pl.ds(half + left, HD)]).astype(bf16)
            qcat[n, :, HD:] = rope(proj[:, pl.ds(left, HD)]).astype(bf16)

        for block in range(length // ROWS):
            rows = pl.ds(block * ROWS, ROWS)
            span = (block + 1) * ROWS
            keys, values = kcat[:span, :], vcat[:span, :]
            position = lax.broadcasted_iota(jnp.int32, (ROWS, ROWS), 0)
            earlier = lax.broadcasted_iota(jnp.int32, (ROWS, ROWS), 1)
            both = [qcat[n, rows, :] for n in pair]
            raw = [mm_nt(both[n][:, HD:], keys[:, :HD]) for n in pair]
            d_raw = [mm_nt(both[n], keys) for n in pair]
            weights, d_scores, low_weights, low_d_weights = [], [], [], []
            for n in pair:
                scores = raw[n] * (scale * math.log2(math.e))
                corner = jnp.where(earlier <= position, scores[:, span - ROWS:], -1e30)
                if block:
                    scores = jnp.concatenate([scores[:, :span - ROWS], corner], axis=1)
                else:
                    scores = corner
                top = jnp.max(scores, axis=1, keepdims=True)
                grown = jnp.exp2(scores - top)
                share = grown * (1.0 / jnp.sum(grown, axis=1, keepdims=True))
                moved = d_raw[n] - jnp.sum(share * d_raw[n], axis=1, keepdims=True)
                weights.append(share)
                d_scores.append(moved)
                low_weights.append(share.astype(bf16))
                low_d_weights.append((share * moved).astype(bf16))
            mixed = [mm(low_weights[n], values) for n in pair]
            d_mixed = [mm(low_d_weights[n], values[:, :HD]) for n in pair]
            miss, d_miss, mean, d_mean = [], [], [], []
            for n in pair:
                mixture = mixed[n][:, :HD]
                target = wanted_ref[rows, n * HD:(n + 1) * HD].astype(f32)
                miss.append((mixture - target).astype(bf16))
                d_miss.append((mixed[n][:, HD:] + d_mixed[n] * scale).astype(bf16))
                miss32, d_miss32 = miss[n].astype(f32), d_miss[n].astype(f32)
                mean.append(jnp.sum(miss32 * mixture, axis=1, keepdims=True))
                d_mean.append(
                    jnp.sum(d_miss32 * mixture + miss32 * d_miss32, axis=1, keepdims=True)
                )
            away = [mm_nt(miss[n], values[:, :HD]) for n in pair]
            d_away = [mm_nt(jnp.concatenate([d_miss[n], miss[n]], axis=1), values) for n in pair]
            back, d_back = [], []
            for n in pair:
                off = away[n] - mean[n]
                back.append((weights[n] * off).astype(bf16))
                d_back.append(
                    (weights[n] * (scale * (d_scores[n] * off) + (d_away[n] - d_mean[n]))).astype(bf16)
                )
            for n in pair:
                dual_q = mm(d_back[n], keys[:, :HD]) + mm(back[n], keys[:, HD:])
                low_ref[rows, pl.ds(pl.multiple_of((2 * head + n) * HD, HD), HD)] = unrope(
                    dual_q * (scale * factor), rows
                ).astype(bf16)
            left_k = [part for n in pair for part in (both[n][:, HD:], both[n][:, :HD])]
            right_k = [part for n in pair for part in (d_back[n], back[n])]
            left_v = [
                part for n in pair
                for part in ((miss[n].astype(f32) * scale).astype(bf16), d_miss[n])
            ]
            right_v = [part for n in pair for part in (low_d_weights[n], low_weights[n])]
            dkt[:, :span] += mm(jnp.concatenate(left_k, axis=0).T, jnp.concatenate(right_k, axis=0))
            dvt[:, :span] += mm(jnp.concatenate(left_v, axis=0).T, jnp.concatenate(right_v, axis=0))

    @pl.when((head == members // 2 - 1) & active)
    def _():
        every = pl.ds(0, length)
        low_ref[:, wide:wide + HD] = unrope(dkt[...].T * (scale * factor), every).astype(bf16)
        low_ref[:, wide + HD:] = (dvt[...].T * factor).astype(bf16)


def attention(wanted, first, width, tables, factor, early=None, features=None, slabs=(), places=None):
    length = wanted.shape[0]
    half = width // 2
    members = half // HD - 2
    first = first // (2 * HD)
    late = len(slabs)
    if places is None:
        places = jnp.ones((1,), jnp.int32)
    slow = pl.BlockSpec(memory_space=pltpu.HBM)
    table = pl.BlockSpec((length, HD), lambda h, p: (0, 0))
    early_spec = [slow if late else pl.BlockSpec((length, width), lambda h, p: (0, 0))]
    scratch = [pltpu.VMEM((length, 2 * HD), jnp.bfloat16)] * 2
    scratch += [pltpu.VMEM((2, length, 2 * HD), jnp.bfloat16)]
    scratch += [pltpu.VMEM((HD, length), jnp.float32)] * 2
    if late:
        depth = late * slabs[0].shape[0]
        scratch += [
            pltpu.VMEM((length, width), jnp.float32),
            pltpu.VMEM((length, depth), jnp.bfloat16),
            pltpu.VMEM((depth, width), jnp.bfloat16),
            pltpu.SemaphoreType.DMA((2 * late + 1,)),
        ]
    return pl.pallas_call(
        functools.partial(attention_kernel, members, factor, late, early is not None),
        grid_spec=pltpu.PrefetchScalarGridSpec(
            num_scalar_prefetch=1,
            grid=(members // 2,),
            in_specs=[slow] * (late + 1 if late else 0)
            + (early_spec if early is not None else [])
            + [pl.BlockSpec((length, 2 * HD), lambda h, p: (0, first + h)), table, table],
            out_specs=pl.BlockSpec((length, half), lambda h, p: (0, 0)),
            scratch_shapes=scratch,
        ),
        out_shape=jax.ShapeDtypeStruct((length, half), jnp.bfloat16),
        compiler_params=pltpu.CompilerParams(
            dimension_semantics=("arbitrary",), vmem_limit_bytes=56 * 2 ** 20
        ),
        cost_estimate=SMALL,
        name="attention_curvature",
    )(places, *((features, *slabs) if late else ()), *(() if early is None else (early,)), wanted, *tables)


def pack_kernel(groups, inputs, *refs):
    parts, outs = refs[:inputs], refs[inputs:]
    for g in range(groups):
        left = 0
        for ref in parts:
            width = ref.shape[1] // groups
            outs[g][:, left:left + width] = ref[:, g * width:(g + 1) * width]
            left += width
    if len(refs) > inputs + groups:
        rows, first, second = refs[-3:]
        first[...] = rows[:, :rows.shape[1] // 2]
        second[...] = rows[:, rows.shape[1] // 2:]


def packed(parts, tokens=None):
    rows = parts[0].shape[0]
    groups = parts[1].shape[1] // HD
    shapes = [(rows, sum(part.shape[1] for part in parts) // groups)] * groups
    inputs = list(parts)
    if tokens is not None:
        inputs.append(tokens)
        shapes += [(tokens.shape[0], tokens.shape[1] // 2)] * 2
    steps = 2

    def block(shape):
        return pl.BlockSpec((shape[0] // steps, shape[1]), lambda i: (i, 0))

    def kernel(*refs):
        count = len(inputs)
        if tokens is None:
            return pack_kernel(groups, count, *refs)
        return pack_kernel(groups, count - 1, *refs[:count - 1], *refs[count:count + groups],
                           refs[count - 1], *refs[count + groups:])

    return pl.pallas_call(
        kernel,
        grid=(steps,),
        in_specs=[block(x.shape) for x in inputs],
        out_specs=[block(shape) for shape in shapes],
        out_shape=[jax.ShapeDtypeStruct(shape, parts[0].dtype) for shape in shapes],
        cost_estimate=SMALL,
        name="pack_rows",
    )(*inputs)


def finish_kernel(inner, total_a, home, crossed, back, out_q, out_k, out_v):
    f32 = jnp.float32
    mine = inner[0] == 1
    total_b = jnp.where(
        mine, home[...].astype(f32) + crossed[...].astype(f32), back[...].astype(f32)
    )
    wide = total_b.shape[1] - 2 * HD
    for n, total in enumerate((total_a[...], total_b)):
        out_q[:, n * wide:(n + 1) * wide] = total[:, :wide]
        out_k[:, n * HD:(n + 1) * HD] = total[:, wide:wide + HD]
        out_v[:, n * HD:(n + 1) * HD] = total[:, wide + HD:]


def finish(inner, *terms):
    rows, width = terms[0].shape
    widths = (2 * (width - 2 * HD), 2 * HD, 2 * HD)
    block = rows // 2
    return pl.pallas_call(
        finish_kernel,
        grid_spec=pltpu.PrefetchScalarGridSpec(
            num_scalar_prefetch=1,
            grid=(2,),
            in_specs=[pl.BlockSpec((block, width), lambda i, p: (i, 0))] * len(terms),
            out_specs=[pl.BlockSpec((block, w), lambda i, p: (i, 0)) for w in widths],
        ),
        out_shape=[jax.ShapeDtypeStruct((rows, w), jnp.float32) for w in widths],
        cost_estimate=SMALL,
        name="finish_sums",
    )(inner.astype(jnp.int32)[None], *terms)


def unpacked(sums):
    wide = sums[0].shape[1] - 2 * HD
    return tuple(
        jnp.concatenate([s[:, lo:hi] for s in sums], axis=1)
        for lo, hi in ((0, wide), (wide, wide + HD), (wide + HD, wide + 2 * HD))
    )


def transposed_product(features, low):
    return lax.dot_general(
        features, low, (((0,), (0,)), ((), ())), preferred_element_type=jnp.float32
    ).astype(jnp.bfloat16)


def by_sequence(tokens, target, *parts):
    length = tokens.shape[0]
    factor = (length * lax.axis_size("fsdp")) ** (-0.5)
    groups = parts[1].shape[1] // HD
    wide = target.shape[1] // groups
    features = lax.all_gather(tokens, "tp", axis=1, tiled=True)
    gathered = [lax.all_gather(rows, "fsdp", axis=0, tiled=True) for rows in packed(parts)]
    tables = rope_tables(length, HD)
    sums = []
    for g in range(groups):
        early = mm(features, gathered[g])
        low = attention(target, g * wide, early.shape[1], tables, factor, early)
        part = transposed_product(features, low)
        sums.append(lax.psum_scatter(part, "fsdp", scatter_dimension=0, tiled=True).astype(jnp.float32))
    return unpacked(sums)


def after(value, *others):
    return lax.optimization_barrier((value,) + others)[0]


def inner_heavy(tokens, target, *parts):
    f32, bf16 = jnp.float32, jnp.bfloat16
    length = tokens.shape[0]
    position = lax.axis_index("fsdp")
    chip, core = position // 2, position % 2
    side, low_high = chip // 2, chip % 2
    inner = (chip == 1) | (chip == 2)
    factor = (length * lax.axis_size("fsdp")) ** (-0.5)
    wide = target.shape[1] // 2

    def chips(pairs):
        return [(2 * a + c, 2 * b + c) for a, b in pairs for c in range(2)]

    swap_sides = chips([(0, 1), (1, 0), (2, 3), (3, 2)])
    inwards, outwards = chips([(0, 1), (3, 2)]), chips([(1, 0), (2, 3)])
    middle, beyond = chips([(1, 2), (2, 1)]), chips([(0, 2), (3, 1)])
    middle_out, ends = chips([(1, 3), (2, 0)]), chips([(0, 3), (3, 0)])
    swap_cores = [(n, n ^ 1) for n in range(8)]

    def along(value, pairs):
        return lax.ppermute(value, "fsdp", pairs)

    def other_core(value):
        return along(value, swap_cores)

    def across(value, bit):
        return lax.ppermute(value, "tp", [(n, n ^ bit) for n in range(4)])

    column = lax.axis_index("tp")
    columns = [column ^ bit for bit in (0, 1, 0, 2, 2, 3, 1, 3)]
    oi, oo = jnp.where(side == 0, 2, 1), jnp.where(side == 0, 3, 0)
    hi, ho = 3 - oi, 3 - oo
    slots = [2 * z + c for z in (chip, chip ^ 1, oi, oo) for c in (core, 1 - core)]

    def places(active, which=range(8)):
        return jnp.stack([active] + [slots[n] for n in which]).astype(jnp.int32)

    def plus(*terms):
        return functools.reduce(jnp.add, [term.astype(f32) for term in terms])

    tables = rope_tables(length, HD)

    phase = lax.optimization_barrier
    own_a, own_b, first, second = packed(parts, tokens)
    width = own_a.shape[1]
    x_first, y_second = across(first, 1), across(second, 2)
    side_a, mid_a, own_a2, *tables = phase(
        (along(own_a, swap_sides), along(own_a, middle), other_core(own_a), *tables)
    )
    outer_tokens = along(after(jnp.stack([first, second]), side_a), inwards)
    firsts, seconds = jnp.stack([first, x_first]), jnp.stack([second, y_second])
    pieces = [firsts, seconds, across(firsts, 2), across(seconds, 1)]
    features, mine_t, theirs_t = place(pieces, columns, core)
    late_side, late_mid = phase((side_a, mid_a, features))[:2]
    far_a, out_a, outer_tokens, side_a2, mid_a2, features = phase(
        (
            along(side_a, middle), along(mid_a, outwards), outer_tokens,
            other_core(late_side), other_core(late_mid), features,
        )
    )
    far_a2, out_a2, own_b = other_core(far_a), other_core(out_a), after(own_b, far_a)
    first, second = phase((outer_tokens[0], outer_tokens[1], far_a2, out_a2))[:2]
    inner_low = attention(
        target, 0, width, tables, factor, None, features,
        [own_a, own_a2, side_a, side_a2, mid_a, mid_a2, far_a, far_a2], places(inner),
    )
    x_first, y_second, out_far_a, mid_b, side_b, inner_low = phase(
        (
            across(first, 1), across(second, 2), along(far_a, outwards), along(own_b, middle),
            along(own_b, inwards), inner_low,
        )
    )
    far_b = along(side_b, middle)
    own_b = after(own_b, inner_low)
    out_far_a2, side_b2 = phase((other_core(out_far_a), other_core(side_b)))
    mid_b, own_b, theirs_t = phase((mid_b, own_b, theirs_t, out_far_a2))[:3]
    first, second, x_first, y_second = phase((first, second, x_first, y_second, out_far_a2))[:4]
    firsts, seconds = jnp.stack([first, x_first]), jnp.stack([second, y_second])
    pieces = [firsts, seconds, across(firsts, 2), across(seconds, 1)]
    mid_b2, own_b2 = other_core(mid_b), other_core(own_b)
    outer_low = attention(
        target, 0, width, tables, factor, None, features,
        [own_a, own_a2, side_a, side_a2, out_a, out_a2, out_far_a, out_far_a2], places(~inner),
    )
    low_a = jnp.where(inner, inner_low, outer_low)
    rows_t, lows = [mine_t, other_core(theirs_t)], [low_a, other_core(low_a)]

    slabs_b = [own_b, own_b2, side_b, side_b2, mid_b, mid_b2]
    early = fold(after(features, low_a), slabs_b, places(inner, range(6)))
    sums = gradient(rows_t, lows, after(jnp.stack([oo, oi, ho, hi]), early), 4)
    far_b, early, sums, pieces = phase((far_b, early, [part[0] for part in sums], pieces))
    away, home = sums[:2], sums[2:]
    far_b2 = other_core(far_b)
    from_inner = along(away[1], middle), along(away[0], middle_out)
    home_swap = along(jnp.where(inner, home[0], home[1]), swap_sides)
    outer_wanted = along(after(target[:, wide:], far_b), inwards)
    own_low = attention(
        target, wide, width, tables, factor, early, features, [far_b, far_b2],
        places(inner, (6, 7)),
    )
    pieces[0] = after(pieces[0], own_low)
    outer_features, mine_t, theirs_t = place(pieces, columns, core)
    from_inner, home_swap, outer_wanted, own_low, outer_features, theirs_t = phase(
        (from_inner, home_swap, outer_wanted, own_low, outer_features, theirs_t)
    )
    away = phase((away, from_inner))[0]
    from_outer = along(away[1], beyond), along(away[0], ends)
    own_low2, theirs_t = other_core(own_low), other_core(theirs_t)
    outer_low = attention(
        outer_wanted, 0, width, tables, factor, None, outer_features,
        slabs_b + [far_b, far_b2], places(inner),
    )
    rows_t += [mine_t, theirs_t]
    lows = [own_low, own_low2, outer_low, other_core(after(outer_low, *from_outer))]
    ready = phase((jnp.stack([oo, oi, ho, hi]), theirs_t, own_low2))[0]
    away_out = gradient(rows_t, lows, ready[:1])[0][0]
    home_out = gradient(rows_t, lows, after(ready[2:3], away_out))[0][0]
    lows[0] = after(lows[0], home_out)
    away_in = gradient(rows_t, lows, ready[1:2])[0][0]
    lows[0] = after(lows[0], away_in)
    home_in = gradient(rows_t, lows, ready[3:])[0][0]
    crossed_out, crossed_in = along(away_out, middle), along(away_in, middle)
    total_a = jnp.where(inner, home[1], home[0]).astype(f32) + plus(
        home_swap, *from_inner, *from_outer
    )
    back_b = along(plus(home_out, crossed_out).astype(bf16), outwards)
    return finish(inner, total_a, home_in, crossed_in, back_b)


def solution(mesh):
    spec = P("fsdp", "tp")

    def shards(*args):
        groups = args[3].shape[1] // HD
        if mesh.shape["fsdp"] == 8 and mesh.shape["tp"] == 4 and groups == 2:
            return tuple(inner_heavy(*args))
        return by_sequence(*args)

    return jax.shard_map(
        shards,
        mesh=mesh,
        in_specs=(spec,) * 8,
        out_specs=(spec,) * 3,
        check_vma=False,
    )
```

```python
import functools
import math

import jax
import jax.numpy as jnp
from jax import lax
from jax.experimental import pallas as pl
from jax.experimental.pallas import tpu as pltpu
from jax.sharding import PartitionSpec as P

HD = 128
SMALL = pl.CostEstimate(flops=1000, bytes_accessed=1000, transcendentals=0)
SIDE = 512
ROWS = 256


def rope_tables(length, width):
    halfway = width // 2
    frequency = jnp.exp(jnp.arange(halfway, dtype=jnp.float32) * (-2.0 * math.log(10000.0) / width))
    angles = jnp.arange(length, dtype=jnp.float32)[:, None] * frequency[None, :]
    cosine, sine = jnp.cos(angles), jnp.sin(angles)
    return jnp.concatenate([cosine, cosine], axis=1), jnp.concatenate([-sine, sine], axis=1)


def mm(a, b):
    return jnp.dot(a, b, preferred_element_type=jnp.float32)


def mm_nt(a, b):
    return lax.dot_general(a, b, (((1,), (1,)), ((), ())), preferred_element_type=jnp.float32)


def slab_copies(places, features, slabs, x_buf, w_buf, sems):
    depth = slabs[0].shape[-2]
    copies = []
    for n, slab in enumerate(slabs):
        here = pl.ds(n * depth, depth)
        column = pl.ds(pl.multiple_of(places[n + 1] * depth, depth), depth)
        copies.append(pltpu.make_async_copy(slab, w_buf.at[here, :], sems.at[2 * n]))
        copies.append(
            pltpu.make_async_copy(features.at[:, column], x_buf.at[:, here], sems.at[2 * n + 1])
        )
    return copies


def project(copies, x_buf, w_buf, out, add):
    depth, width = w_buf.shape
    slabs = len(copies) // 2
    cuts = [0, slabs] if slabs == 2 else [0, 2, slabs]
    for copy in copies[:2 * cuts[1]]:
        copy.start()
    for n in range(len(cuts) - 1):
        for copy in copies[2 * cuts[n]:2 * cuts[n + 1]]:
            copy.wait()
        if n + 2 < len(cuts):
            for copy in copies[2 * cuts[n + 1]:]:
                copy.start()
        ks = slice(cuts[n] * depth // slabs, cuts[n + 1] * depth // slabs)
        for left in range(0, width, SIDE):
            columns = pl.ds(left, SIDE)
            total = mm(x_buf[:, ks], w_buf[ks, columns])
            if n or add:
                total += out[:, columns]
            out[:, columns] = total


def fold_kernel(pairs, places, *refs):
    x_buf, w_buf, sems = refs[pairs + 2:]

    @pl.when(places[0] == 1)
    def _():
        copies = slab_copies(places, refs[0], refs[1:pairs + 1], x_buf, w_buf, sems)
        project(copies, x_buf, w_buf, refs[pairs + 1], False)


def fold(features, slabs, places):
    rows = features.shape[0]
    depth, width = slabs[0].shape
    pairs = len(slabs)
    slow = pl.BlockSpec(memory_space=pltpu.HBM)
    return pl.pallas_call(
        functools.partial(fold_kernel, pairs),
        grid_spec=pltpu.PrefetchScalarGridSpec(
            num_scalar_prefetch=1,
            grid=(),
            in_specs=[slow] * (pairs + 1),
            out_specs=pl.BlockSpec((rows, width), lambda p: (0, 0)),
            scratch_shapes=[
                pltpu.VMEM((rows, pairs * depth), jnp.bfloat16),
                pltpu.VMEM((pairs * depth, width), jnp.bfloat16),
                pltpu.SemaphoreType.DMA((2 * pairs,)),
            ],
        ),
        out_shape=jax.ShapeDtypeStruct((rows, width), jnp.float32),
        compiler_params=pltpu.CompilerParams(vmem_limit_bytes=48 * 2 ** 20),
        cost_estimate=SMALL,
        name="fold_projections",
    )(places, features, *slabs)


def place_kernel(places, *refs):
    pieces, (out, mine, theirs) = refs[:-3], refs[-3:]
    for n, ref in enumerate(pieces):

        @pl.when(pl.program_id(0) // 2 == n)
        def _():
            out[...] = ref[0]
            turned = ref[0].T
            mine[...] = turned
            theirs[...] = turned


def place(stacks, columns, core):
    rows, width = stacks[0].shape[1:]
    count = 2 * len(stacks)
    half = [n // 2 % 2 for n in range(count)]
    spare = len(stacks)
    tables = [
        [2 * columns[n] + half[n] for n in range(count)],
        [jnp.where(core == half[n], columns[n], spare) for n in range(count)],
        [jnp.where(core == half[n], spare, columns[n]) for n in range(count)],
    ]
    tables = jnp.stack([jnp.stack(table) for table in tables]).astype(jnp.int32)

    def piece(n):
        return pl.BlockSpec((1, rows, width), lambda i, p: (jnp.clip(i - 2 * n, 0, 1), 0, 0))

    return pl.pallas_call(
        place_kernel,
        grid_spec=pltpu.PrefetchScalarGridSpec(
            num_scalar_prefetch=1,
            grid=(count,),
            in_specs=[piece(n) for n in range(len(stacks))],
            out_specs=[
                pl.BlockSpec((rows, width), lambda i, p: (0, p[0, i])),
                pl.BlockSpec((width, rows), lambda i, p: (p[1, i], 0)),
                pl.BlockSpec((width, rows), lambda i, p: (p[2, i], 0)),
            ],
        ),
        out_shape=[pltpu.HBM((rows, count * width), stacks[0].dtype)]
        + [pltpu.HBM(((spare + 1) * width, rows), stacks[0].dtype)] * 2,
        compiler_params=pltpu.CompilerParams(
            dimension_semantics=("arbitrary",), vmem_limit_bytes=32 * 2 ** 20
        ),
        cost_estimate=SMALL,
        name="place_tokens",
    )(tables, *stacks)


def gradient_kernel(pairs, outs, _, *refs):
    total = None
    for n in range(pairs):
        term = mm(refs[n][...], refs[pairs + n][...])
        total = term if total is None else total + term
    each = pl.num_programs(0) // outs
    for n in range(outs):

        @pl.when(pl.program_id(0) // each == n)
        def _():
            refs[2 * pairs + n][0] = total.astype(jnp.bfloat16)


def gradient(features, lows, blocks, outs=1):
    length, width = lows[0].shape
    depth = features[0].shape[0] // 5
    pairs, count = len(features), blocks.shape[0]
    each = count // outs

    def part(n):
        return pl.BlockSpec(
            (1, depth, width), lambda i, p: (jnp.clip(i - n * each, 0, each - 1), 0, 0)
        )

    return pl.pallas_call(
        functools.partial(gradient_kernel, pairs, outs),
        grid_spec=pltpu.PrefetchScalarGridSpec(
            num_scalar_prefetch=1,
            grid=(count,),
            in_specs=[pl.BlockSpec((depth, length), lambda i, p: (p[i], 0))] * pairs
            + [pl.BlockSpec((length, width), lambda i, p: (0, 0))] * pairs,
            out_specs=[part(n) for n in range(outs)],
        ),
        out_shape=[jax.ShapeDtypeStruct((each, depth, width), jnp.bfloat16)] * outs,
        compiler_params=pltpu.CompilerParams(
            dimension_semantics=("arbitrary",), vmem_limit_bytes=48 * 2 ** 20
        ),
        cost_estimate=SMALL,
        name="gradient_rows",
    )(blocks, *features, *lows)


def attention_kernel(members, factor, late, has_early, places, *refs):
    features, refs = (refs[0], refs[1:]) if late else (None, refs)
    slabs, refs = refs[:late], refs[late:]
    early_ref, refs = (refs[0], refs[1:]) if has_early else (None, refs)
    wanted_ref, cos_ref, sin_ref, low_ref, kcat, vcat, qcat, dkt, dvt = refs[:9]
    proj, x_buf, w_buf, sems = refs[9:] if late else (early_ref, None, None, None)
    head = pl.program_id(0)
    length = cos_ref.shape[0]
    wide = members * HD
    half = wide + 2 * HD
    scale = HD ** -0.5
    bf16, f32 = jnp.bfloat16, jnp.float32

    def rope(u):
        return u * cos_ref[...] + pltpu.roll(u, HD // 2, 1) * sin_ref[...]

    def unrope(u, rows):
        return u * cos_ref[rows, :] - pltpu.roll(u, HD // 2, 1) * sin_ref[rows, :]

    active = places[0] == 1

    @pl.when((head == 0) & (places[0] == 0))
    def _():
        low_ref[...] = jnp.zeros_like(low_ref)

    @pl.when((head == 0) & active)
    def _():
        if late:
            copies = slab_copies(places, features, slabs, x_buf, w_buf, sems)
            if has_early:
                fetched = pltpu.make_async_copy(early_ref, proj, sems.at[2 * late])
                fetched.start()
                fetched.wait()
            project(copies, x_buf, w_buf, proj, has_early)
        kcat[:, :HD] = rope(proj[:, wide:wide + HD]).astype(bf16)
        kcat[:, HD:] = rope(proj[:, half + wide:half + wide + HD]).astype(bf16)
        vcat[:, :HD] = proj[:, wide + HD:half].astype(bf16)
        vcat[:, HD:] = proj[:, half + wide + HD:].astype(bf16)
        dkt[...] = jnp.zeros_like(dkt)
        dvt[...] = jnp.zeros_like(dvt)

    @pl.when(active)
    def _():
        pair = range(2)
        for n in pair:
            left = pl.multiple_of((2 * head + n) * HD, HD)
            qcat[n, :, :HD] = rope(proj[:, pl.ds(half + left, HD)]).astype(bf16)
            qcat[n, :, HD:] = rope(proj[:, pl.ds(left, HD)]).astype(bf16)

        for block in range(length // ROWS):
            rows = pl.ds(block * ROWS, ROWS)
            span = (block + 1) * ROWS
            keys, values = kcat[:span, :], vcat[:span, :]
            position = lax.broadcasted_iota(jnp.int32, (ROWS, ROWS), 0)
            earlier = lax.broadcasted_iota(jnp.int32, (ROWS, ROWS), 1)
            both = [qcat[n, rows, :] for n in pair]
            raw = [mm_nt(both[n][:, HD:], keys[:, :HD]) for n in pair]
            d_raw = [mm_nt(both[n], keys) for n in pair]
            weights, d_scores, low_weights, low_d_weights = [], [], [], []
            for n in pair:
                scores = raw[n] * (scale * math.log2(math.e))
                corner = jnp.where(earlier <= position, scores[:, span - ROWS:], -1e30)
                if block:
                    scores = jnp.concatenate([scores[:, :span - ROWS], corner], axis=1)
                else:
                    scores = corner
                top = jnp.max(scores, axis=1, keepdims=True)
                grown = jnp.exp2(scores - top)
                share = grown * (1.0 / jnp.sum(grown, axis=1, keepdims=True))
                moved = d_raw[n] - jnp.sum(share * d_raw[n], axis=1, keepdims=True)
                weights.append(share)
                d_scores.append(moved)
                low_weights.append(share.astype(bf16))
                low_d_weights.append((share * moved).astype(bf16))
            mixed = [mm(low_weights[n], values) for n in pair]
            d_mixed = [mm(low_d_weights[n], values[:, :HD]) for n in pair]
            miss, d_miss, mean, d_mean = [], [], [], []
            for n in pair:
                mixture = mixed[n][:, :HD]
                target = wanted_ref[rows, n * HD:(n + 1) * HD].astype(f32)
                miss.append((mixture - target).astype(bf16))
                d_miss.append((mixed[n][:, HD:] + d_mixed[n] * scale).astype(bf16))
                miss32, d_miss32 = miss[n].astype(f32), d_miss[n].astype(f32)
                mean.append(jnp.sum(miss32 * mixture, axis=1, keepdims=True))
                d_mean.append(
                    jnp.sum(d_miss32 * mixture + miss32 * d_miss32, axis=1, keepdims=True)
                )
            away = [mm_nt(miss[n], values[:, :HD]) for n in pair]
            d_away = [mm_nt(jnp.concatenate([d_miss[n], miss[n]], axis=1), values) for n in pair]
            back, d_back = [], []
            for n in pair:
                off = away[n] - mean[n]
                back.append((weights[n] * off).astype(bf16))
                d_back.append(
                    (weights[n] * (scale * (d_scores[n] * off) + (d_away[n] - d_mean[n]))).astype(bf16)
                )
            for n in pair:
                dual_q = mm(d_back[n], keys[:, :HD]) + mm(back[n], keys[:, HD:])
                low_ref[rows, pl.ds(pl.multiple_of((2 * head + n) * HD, HD), HD)] = unrope(
                    dual_q * (scale * factor), rows
                ).astype(bf16)
            left_k = [part for n in pair for part in (both[n][:, HD:], both[n][:, :HD])]
            right_k = [part for n in pair for part in (d_back[n], back[n])]
            left_v = [
                part for n in pair
                for part in ((miss[n].astype(f32) * scale).astype(bf16), d_miss[n])
            ]
            right_v = [part for n in pair for part in (low_d_weights[n], low_weights[n])]
            dkt[:, :span] += mm(jnp.concatenate(left_k, axis=0).T, jnp.concatenate(right_k, axis=0))
            dvt[:, :span] += mm(jnp.concatenate(left_v, axis=0).T, jnp.concatenate(right_v, axis=0))

    @pl.when((head == members // 2 - 1) & active)
    def _():
        every = pl.ds(0, length)
        low_ref[:, wide:wide + HD] = unrope(dkt[...].T * (scale * factor), every).astype(bf16)
        low_ref[:, wide + HD:] = (dvt[...].T * factor).astype(bf16)


def attention(wanted, first, width, tables, factor, early=None, features=None, slabs=(), places=None):
    length = wanted.shape[0]
    half = width // 2
    members = half // HD - 2
    first = first // (2 * HD)
    late = len(slabs)
    if places is None:
        places = jnp.ones((1,), jnp.int32)
    slow = pl.BlockSpec(memory_space=pltpu.HBM)
    table = pl.BlockSpec((length, HD), lambda h, p: (0, 0))
    early_spec = [slow if late else pl.BlockSpec((length, width), lambda h, p: (0, 0))]
    scratch = [pltpu.VMEM((length, 2 * HD), jnp.bfloat16)] * 2
    scratch += [pltpu.VMEM((2, length, 2 * HD), jnp.bfloat16)]
    scratch += [pltpu.VMEM((HD, length), jnp.float32)] * 2
    if late:
        depth = late * slabs[0].shape[0]
        scratch += [
            pltpu.VMEM((length, width), jnp.float32),
            pltpu.VMEM((length, depth), jnp.bfloat16),
            pltpu.VMEM((depth, width), jnp.bfloat16),
            pltpu.SemaphoreType.DMA((2 * late + 1,)),
        ]
    return pl.pallas_call(
        functools.partial(attention_kernel, members, factor, late, early is not None),
        grid_spec=pltpu.PrefetchScalarGridSpec(
            num_scalar_prefetch=1,
            grid=(members // 2,),
            in_specs=[slow] * (late + 1 if late else 0)
            + (early_spec if early is not None else [])
            + [pl.BlockSpec((length, 2 * HD), lambda h, p: (0, first + h)), table, table],
            out_specs=pl.BlockSpec((length, half), lambda h, p: (0, 0)),
            scratch_shapes=scratch,
        ),
        out_shape=jax.ShapeDtypeStruct((length, half), jnp.bfloat16),
        compiler_params=pltpu.CompilerParams(
            dimension_semantics=("arbitrary",), vmem_limit_bytes=56 * 2 ** 20
        ),
        cost_estimate=SMALL,
        name="attention_curvature",
    )(places, *((features, *slabs) if late else ()), *(() if early is None else (early,)), wanted, *tables)


def pack_kernel(groups, inputs, *refs):
    parts, outs = refs[:inputs], refs[inputs:]
    for g in range(groups):
        left = 0
        for ref in parts:
            width = ref.shape[1] // groups
            outs[g][:, left:left + width] = ref[:, g * width:(g + 1) * width]
            left += width
    if len(refs) > inputs + groups:
        rows, first, second = refs[-3:]
        first[...] = rows[:, :rows.shape[1] // 2]
        second[...] = rows[:, rows.shape[1] // 2:]


def packed(parts, tokens=None):
    rows = parts[0].shape[0]
    groups = parts[1].shape[1] // HD
    shapes = [(rows, sum(part.shape[1] for part in parts) // groups)] * groups
    inputs = list(parts)
    if tokens is not None:
        inputs.append(tokens)
        shapes += [(tokens.shape[0], tokens.shape[1] // 2)] * 2
    steps = 2

    def block(shape):
        return pl.BlockSpec((shape[0] // steps, shape[1]), lambda i: (i, 0))

    def kernel(*refs):
        count = len(inputs)
        if tokens is None:
            return pack_kernel(groups, count, *refs)
        return pack_kernel(groups, count - 1, *refs[:count - 1], *refs[count:count + groups],
                           refs[count - 1], *refs[count + groups:])

    return pl.pallas_call(
        kernel,
        grid=(steps,),
        in_specs=[block(x.shape) for x in inputs],
        out_specs=[block(shape) for shape in shapes],
        out_shape=[jax.ShapeDtypeStruct(shape, parts[0].dtype) for shape in shapes],
        cost_estimate=SMALL,
        name="pack_rows",
    )(*inputs)


def finish_kernel(inner, total_a, home, crossed, back, out_q, out_k, out_v):
    f32 = jnp.float32
    mine = inner[0] == 1
    total_b = jnp.where(
        mine, home[...].astype(f32) + crossed[...].astype(f32), back[...].astype(f32)
    )
    wide = total_b.shape[1] - 2 * HD
    for n, total in enumerate((total_a[...], total_b)):
        out_q[:, n * wide:(n + 1) * wide] = total[:, :wide]
        out_k[:, n * HD:(n + 1) * HD] = total[:, wide:wide + HD]
        out_v[:, n * HD:(n + 1) * HD] = total[:, wide + HD:]


def finish(inner, *terms):
    rows, width = terms[0].shape
    widths = (2 * (width - 2 * HD), 2 * HD, 2 * HD)
    block = rows // 2
    return pl.pallas_call(
        finish_kernel,
        grid_spec=pltpu.PrefetchScalarGridSpec(
            num_scalar_prefetch=1,
            grid=(2,),
            in_specs=[pl.BlockSpec((block, width), lambda i, p: (i, 0))] * len(terms),
            out_specs=[pl.BlockSpec((block, w), lambda i, p: (i, 0)) for w in widths],
        ),
        out_shape=[jax.ShapeDtypeStruct((rows, w), jnp.float32) for w in widths],
        cost_estimate=SMALL,
        name="finish_sums",
    )(inner.astype(jnp.int32)[None], *terms)


def unpacked(sums):
    wide = sums[0].shape[1] - 2 * HD
    return tuple(
        jnp.concatenate([s[:, lo:hi] for s in sums], axis=1)
        for lo, hi in ((0, wide), (wide, wide + HD), (wide + HD, wide + 2 * HD))
    )


def transposed_product(features, low):
    return lax.dot_general(
        features, low, (((0,), (0,)), ((), ())), preferred_element_type=jnp.float32
    ).astype(jnp.bfloat16)


def by_sequence(tokens, target, *parts):
    length = tokens.shape[0]
    factor = (length * lax.axis_size("fsdp")) ** (-0.5)
    groups = parts[1].shape[1] // HD
    wide = target.shape[1] // groups
    features = lax.all_gather(tokens, "tp", axis=1, tiled=True)
    gathered = [lax.all_gather(rows, "fsdp", axis=0, tiled=True) for rows in packed(parts)]
    tables = rope_tables(length, HD)
    sums = []
    for g in range(groups):
        early = mm(features, gathered[g])
        low = attention(target, g * wide, early.shape[1], tables, factor, early)
        part = transposed_product(features, low)
        sums.append(lax.psum_scatter(part, "fsdp", scatter_dimension=0, tiled=True).astype(jnp.float32))
    return unpacked(sums)


def after(value, *others):
    return lax.optimization_barrier((value,) + others)[0]


def inner_heavy(tokens, target, *parts):
    f32, bf16 = jnp.float32, jnp.bfloat16
    length = tokens.shape[0]
    position = lax.axis_index("fsdp")
    chip, core = position // 2, position % 2
    side, low_high = chip // 2, chip % 2
    inner = (chip == 1) | (chip == 2)
    factor = (length * lax.axis_size("fsdp")) ** (-0.5)
    wide = target.shape[1] // 2

    def chips(pairs):
        return [(2 * a + c, 2 * b + c) for a, b in pairs for c in range(2)]

    swap_sides = chips([(0, 1), (1, 0), (2, 3), (3, 2)])
    inwards, outwards = chips([(0, 1), (3, 2)]), chips([(1, 0), (2, 3)])
    middle, beyond = chips([(1, 2), (2, 1)]), chips([(0, 2), (3, 1)])
    middle_out, ends = chips([(1, 3), (2, 0)]), chips([(0, 3), (3, 0)])
    swap_cores = [(n, n ^ 1) for n in range(8)]

    def along(value, pairs):
        return lax.ppermute(value, "fsdp", pairs)

    def other_core(value):
        return along(value, swap_cores)

    def across(value, bit):
        return lax.ppermute(value, "tp", [(n, n ^ bit) for n in range(4)])

    column = lax.axis_index("tp")
    columns = [column ^ bit for bit in (0, 1, 0, 2, 2, 3, 1, 3)]
    oi, oo = jnp.where(side == 0, 2, 1), jnp.where(side == 0, 3, 0)
    hi, ho = 3 - oi, 3 - oo
    slots = [2 * z + c for z in (chip, chip ^ 1, oi, oo) for c in (core, 1 - core)]

    def places(active, which=range(8)):
        return jnp.stack([active] + [slots[n] for n in which]).astype(jnp.int32)

    def plus(*terms):
        return functools.reduce(jnp.add, [term.astype(f32) for term in terms])

    tables = rope_tables(length, HD)

    phase = lax.optimization_barrier
    own_a, own_b, first, second = packed(parts, tokens)
    width = own_a.shape[1]
    x_first, y_second = across(first, 1), across(second, 2)
    side_a, mid_a, own_a2, *tables = phase(
        (along(own_a, swap_sides), along(own_a, middle), other_core(own_a), *tables)
    )
    outer_tokens = along(after(jnp.stack([first, second]), side_a), inwards)
    firsts, seconds = jnp.stack([first, x_first]), jnp.stack([second, y_second])
    pieces = [firsts, seconds, across(firsts, 2), across(seconds, 1)]
    features, mine_t, theirs_t = place(pieces, columns, core)
    late_side, late_mid = phase((side_a, mid_a, features))[:2]
    far_a, out_a, outer_tokens, side_a2, mid_a2, features = phase(
        (
            along(side_a, middle), along(mid_a, outwards), outer_tokens,
            other_core(late_side), other_core(late_mid), features,
        )
    )
    far_a2, out_a2, own_b = other_core(far_a), other_core(out_a), after(own_b, far_a)
    first, second = phase((outer_tokens[0], outer_tokens[1], far_a2, out_a2))[:2]
    def only(flag, call, dtype):
        shape = (length, width // 2 if dtype == bf16 else width)
        return lax.cond(flag, call, lambda: jnp.zeros(shape, dtype))

    near = [own_a, own_a2, side_a, side_a2]
    inner_low = only(
        inner,
        lambda: attention(
            target, 0, width, tables, factor, None, features,
            near + [mid_a, mid_a2, far_a, far_a2], places(1),
        ),
        bf16,
    )
    early_a = only(
        ~inner, lambda: fold(features, near + [out_a, out_a2], places(1, range(6))), f32
    )
    x_first, y_second, out_far_a, mid_b, side_b, inner_low, early_a = phase(
        (
            across(first, 1), across(second, 2), along(far_a, outwards), along(own_b, middle),
            along(own_b, inwards), inner_low, early_a,
        )
    )
    far_b = along(side_b, middle)
    own_b = after(own_b, inner_low)
    out_far_a2, side_b2 = phase((other_core(out_far_a), other_core(side_b)))
    mid_b, own_b, theirs_t = phase((mid_b, own_b, theirs_t, out_far_a2))[:3]
    first, second, x_first, y_second = phase((first, second, x_first, y_second, out_far_a2))[:4]
    firsts, seconds = jnp.stack([first, x_first]), jnp.stack([second, y_second])
    pieces = [firsts, seconds, across(firsts, 2), across(seconds, 1)]
    mid_b2, own_b2 = other_core(mid_b), other_core(own_b)
    low_a = lax.cond(
        inner,
        lambda: inner_low,
        lambda: attention(
            target, 0, width, tables, factor, early_a, features, [out_far_a, out_far_a2],
            places(1, (6, 7)),
        ),
    )
    rows_t, lows = [mine_t, other_core(theirs_t)], [low_a, other_core(low_a)]

    slabs_b = [own_b, own_b2, side_b, side_b2, mid_b, mid_b2]
    early = fold(after(features, low_a), slabs_b, places(inner, range(6)))
    sums = gradient(rows_t, lows, after(jnp.stack([oo, oi, ho, hi]), early), 4)
    far_b, early, sums, pieces = phase((far_b, early, [part[0] for part in sums], pieces))
    away, home = sums[:2], sums[2:]
    far_b2 = other_core(far_b)
    from_inner = along(away[1], middle), along(away[0], middle_out)
    home_swap = along(jnp.where(inner, home[0], home[1]), swap_sides)
    outer_wanted = along(after(target[:, wide:], far_b), inwards)
    own_low = attention(
        target, wide, width, tables, factor, early, features, [far_b, far_b2],
        places(inner, (6, 7)),
    )
    pieces[0] = after(pieces[0], own_low)
    outer_features, mine_t, theirs_t = place(pieces, columns, core)
    from_inner, home_swap, outer_wanted, own_low, outer_features, theirs_t = phase(
        (from_inner, home_swap, outer_wanted, own_low, outer_features, theirs_t)
    )
    away = phase((away, from_inner))[0]
    from_outer = along(away[1], beyond), along(away[0], ends)
    own_low2, theirs_t = other_core(own_low), other_core(theirs_t)
    outer_low = attention(
        outer_wanted, 0, width, tables, factor, None, outer_features,
        slabs_b + [far_b, far_b2], places(inner),
    )
    rows_t += [mine_t, theirs_t]
    lows = [own_low, own_low2, outer_low, other_core(after(outer_low, *from_outer))]
    ready = phase((jnp.stack([oo, oi, ho, hi]), theirs_t, own_low2))[0]
    away_out = gradient(rows_t, lows, ready[:1])[0][0]
    home_out = gradient(rows_t, lows, after(ready[2:3], away_out))[0][0]
    lows[0] = after(lows[0], home_out)
    away_in = gradient(rows_t, lows, ready[1:2])[0][0]
    lows[0] = after(lows[0], away_in)
    home_in = gradient(rows_t, lows, ready[3:])[0][0]
    crossed_out, crossed_in = along(away_out, middle), along(away_in, middle)
    total_a = jnp.where(inner, home[1], home[0]).astype(f32) + plus(
        home_swap, *from_inner, *from_outer
    )
    back_b = along(plus(home_out, crossed_out).astype(bf16), outwards)
    return finish(inner, total_a, home_in, crossed_in, back_b)


def solution(mesh):
    spec = P("fsdp", "tp")

    def shards(*args):
        groups = args[3].shape[1] // HD
        if mesh.shape["fsdp"] == 8 and mesh.shape["tp"] == 4 and groups == 2:
            return tuple(inner_heavy(*args))
        return by_sequence(*args)

    return jax.shard_map(
        shards,
        mesh=mesh,
        in_specs=(spec,) * 8,
        out_specs=(spec,) * 3,
        check_vma=False,
    )
```

```python
import functools
import math

import jax
import jax.numpy as jnp
from jax import lax
from jax.experimental import pallas as pl
from jax.experimental.pallas import tpu as pltpu
from jax.sharding import PartitionSpec as P

HD = 128
SMALL = pl.CostEstimate(flops=1000, bytes_accessed=1000, transcendentals=0)
SIDE = 512
ROWS = 256


def rope_tables(length, width):
    halfway = width // 2
    frequency = jnp.exp(jnp.arange(halfway, dtype=jnp.float32) * (-2.0 * math.log(10000.0) / width))
    angles = jnp.arange(length, dtype=jnp.float32)[:, None] * frequency[None, :]
    cosine, sine = jnp.cos(angles), jnp.sin(angles)
    return jnp.concatenate([cosine, cosine], axis=1), jnp.concatenate([-sine, sine], axis=1)


def mm(a, b):
    return jnp.dot(a, b, preferred_element_type=jnp.float32)


def mm_nt(a, b):
    return lax.dot_general(a, b, (((1,), (1,)), ((), ())), preferred_element_type=jnp.float32)


def blank(shape, dtype):
    return pl.pallas_call(
        lambda out: None,
        out_specs=pl.BlockSpec(memory_space=pltpu.HBM),
        out_shape=pltpu.HBM(shape, dtype),
        cost_estimate=SMALL,
        name="blank",
    )()


def slab_copies(places, features, slabs, x_buf, w_buf, sems):
    depth = slabs[0].shape[-2]
    copies = []
    for n, slab in enumerate(slabs):
        here = pl.ds(n * depth, depth)
        column = pl.ds(pl.multiple_of(places[n + 1] * depth, depth), depth)
        copies.append(pltpu.make_async_copy(slab, w_buf.at[here, :], sems.at[2 * n]))
        copies.append(
            pltpu.make_async_copy(features.at[:, column], x_buf.at[:, here], sems.at[2 * n + 1])
        )
    return copies


def project(copies, x_buf, w_buf, out, add):
    depth, width = w_buf.shape
    slabs = len(copies) // 2
    cuts = [0, slabs] if slabs == 2 else [0, 2, slabs]
    for copy in copies[:2 * cuts[1]]:
        copy.start()
    for n in range(len(cuts) - 1):
        for copy in copies[2 * cuts[n]:2 * cuts[n + 1]]:
            copy.wait()
        if n + 2 < len(cuts):
            for copy in copies[2 * cuts[n + 1]:]:
                copy.start()
        ks = slice(cuts[n] * depth // slabs, cuts[n + 1] * depth // slabs)
        for left in range(0, width, SIDE):
            columns = pl.ds(left, SIDE)
            total = mm(x_buf[:, ks], w_buf[ks, columns])
            if n or add:
                total += out[:, columns]
            out[:, columns] = total


def fold_kernel(pairs, places, *refs):
    x_buf, w_buf, sems = refs[pairs + 2:]

    @pl.when(places[0] == 1)
    def _():
        copies = slab_copies(places, refs[0], refs[1:pairs + 1], x_buf, w_buf, sems)
        project(copies, x_buf, w_buf, refs[pairs + 1], False)


def fold(features, slabs, places):
    rows = features.shape[0]
    depth, width = slabs[0].shape
    pairs = len(slabs)
    slow = pl.BlockSpec(memory_space=pltpu.HBM)
    return pl.pallas_call(
        functools.partial(fold_kernel, pairs),
        grid_spec=pltpu.PrefetchScalarGridSpec(
            num_scalar_prefetch=1,
            grid=(),
            in_specs=[slow] * (pairs + 1),
            out_specs=pl.BlockSpec((rows, width), lambda p: (0, 0)),
            scratch_shapes=[
                pltpu.VMEM((rows, pairs * depth), jnp.bfloat16),
                pltpu.VMEM((pairs * depth, width), jnp.bfloat16),
                pltpu.SemaphoreType.DMA((2 * pairs,)),
            ],
        ),
        out_shape=jax.ShapeDtypeStruct((rows, width), jnp.float32),
        compiler_params=pltpu.CompilerParams(vmem_limit_bytes=48 * 2 ** 20),
        cost_estimate=SMALL,
        name="fold_projections",
    )(places, features, *slabs)


def place_kernel(places, *refs):
    pieces, (out, mine, theirs) = refs[:-3], refs[-3:]
    for n, ref in enumerate(pieces):

        @pl.when(pl.program_id(0) // 2 == n)
        def _():
            out[...] = ref[0]
            turned = ref[0].T
            mine[...] = turned
            theirs[...] = turned


def place(stacks, columns, core):
    rows, width = stacks[0].shape[1:]
    count = 2 * len(stacks)
    half = [n // 2 % 2 for n in range(count)]
    spare = len(stacks)
    tables = [
        [2 * columns[n] + half[n] for n in range(count)],
        [jnp.where(core == half[n], columns[n], spare) for n in range(count)],
        [jnp.where(core == half[n], spare, columns[n]) for n in range(count)],
    ]
    tables = jnp.stack([jnp.stack(table) for table in tables]).astype(jnp.int32)

    def piece(n):
        return pl.BlockSpec((1, rows, width), lambda i, p: (jnp.clip(i - 2 * n, 0, 1), 0, 0))

    return pl.pallas_call(
        place_kernel,
        grid_spec=pltpu.PrefetchScalarGridSpec(
            num_scalar_prefetch=1,
            grid=(count,),
            in_specs=[piece(n) for n in range(len(stacks))],
            out_specs=[
                pl.BlockSpec((rows, width), lambda i, p: (0, p[0, i])),
                pl.BlockSpec((width, rows), lambda i, p: (p[1, i], 0)),
                pl.BlockSpec((width, rows), lambda i, p: (p[2, i], 0)),
            ],
        ),
        out_shape=[pltpu.HBM((rows, count * width), stacks[0].dtype)]
        + [pltpu.HBM(((spare + 1) * width, rows), stacks[0].dtype)] * 2,
        compiler_params=pltpu.CompilerParams(
            dimension_semantics=("arbitrary",), vmem_limit_bytes=32 * 2 ** 20
        ),
        cost_estimate=SMALL,
        name="place_tokens",
    )(tables, *stacks)


def gradient_kernel(pairs, outs, _, *refs):
    total = None
    for n in range(pairs):
        term = mm(refs[n][...], refs[pairs + n][...])
        total = term if total is None else total + term
    each = pl.num_programs(0) // outs
    for n in range(outs):

        @pl.when(pl.program_id(0) // each == n)
        def _():
            refs[2 * pairs + n][0] = total.astype(jnp.bfloat16)


def gradient(features, lows, blocks, outs=1):
    length, width = lows[0].shape
    depth = features[0].shape[0] // 5
    pairs, count = len(features), blocks.shape[0]
    each = count // outs

    def part(n):
        return pl.BlockSpec(
            (1, depth, width), lambda i, p: (jnp.clip(i - n * each, 0, each - 1), 0, 0)
        )

    return pl.pallas_call(
        functools.partial(gradient_kernel, pairs, outs),
        grid_spec=pltpu.PrefetchScalarGridSpec(
            num_scalar_prefetch=1,
            grid=(count,),
            in_specs=[pl.BlockSpec((depth, length), lambda i, p: (p[i], 0))] * pairs
            + [pl.BlockSpec((length, width), lambda i, p: (0, 0))] * pairs,
            out_specs=[part(n) for n in range(outs)],
        ),
        out_shape=[jax.ShapeDtypeStruct((each, depth, width), jnp.bfloat16)] * outs,
        compiler_params=pltpu.CompilerParams(
            dimension_semantics=("arbitrary",), vmem_limit_bytes=48 * 2 ** 20
        ),
        cost_estimate=SMALL,
        name="gradient_rows",
    )(blocks, *features, *lows)


def attention_kernel(members, factor, late, has_early, places, *refs):
    features, refs = (refs[0], refs[1:]) if late else (None, refs)
    slabs, refs = refs[:late], refs[late:]
    early_ref, refs = (refs[0], refs[1:]) if has_early else (None, refs)
    wanted_ref, cos_ref, sin_ref, low_ref, kcat, vcat, qcat, dkt, dvt = refs[:9]
    proj, x_buf, w_buf, sems = refs[9:] if late else (early_ref, None, None, None)
    head = pl.program_id(0)
    length = cos_ref.shape[0]
    wide = members * HD
    half = wide + 2 * HD
    scale = HD ** -0.5
    bf16, f32 = jnp.bfloat16, jnp.float32

    def rope(u):
        return u * cos_ref[...] + pltpu.roll(u, HD // 2, 1) * sin_ref[...]

    def unrope(u, rows):
        return u * cos_ref[rows, :] - pltpu.roll(u, HD // 2, 1) * sin_ref[rows, :]

    active = places[0] == 1

    @pl.when((head == 0) & (places[0] == 0))
    def _():
        low_ref[...] = jnp.zeros_like(low_ref)

    @pl.when((head == 0) & active)
    def _():
        if late:
            copies = slab_copies(places, features, slabs, x_buf, w_buf, sems)
            if has_early:
                fetched = pltpu.make_async_copy(early_ref, proj, sems.at[2 * late])
                fetched.start()
                fetched.wait()
            project(copies, x_buf, w_buf, proj, has_early)
        kcat[:, :HD] = rope(proj[:, wide:wide + HD]).astype(bf16)
        kcat[:, HD:] = rope(proj[:, half + wide:half + wide + HD]).astype(bf16)
        vcat[:, :HD] = proj[:, wide + HD:half].astype(bf16)
        vcat[:, HD:] = proj[:, half + wide + HD:].astype(bf16)
        dkt[...] = jnp.zeros_like(dkt)
        dvt[...] = jnp.zeros_like(dvt)

    @pl.when(active)
    def _():
        pair = range(2)
        for n in pair:
            left = pl.multiple_of((2 * head + n) * HD, HD)
            qcat[n, :, :HD] = rope(proj[:, pl.ds(half + left, HD)]).astype(bf16)
            qcat[n, :, HD:] = rope(proj[:, pl.ds(left, HD)]).astype(bf16)

        for block in range(length // ROWS):
            rows = pl.ds(block * ROWS, ROWS)
            span = (block + 1) * ROWS
            keys, values = kcat[:span, :], vcat[:span, :]
            position = lax.broadcasted_iota(jnp.int32, (ROWS, ROWS), 0)
            earlier = lax.broadcasted_iota(jnp.int32, (ROWS, ROWS), 1)
            both = [qcat[n, rows, :] for n in pair]
            raw = [mm_nt(both[n][:, HD:], keys[:, :HD]) for n in pair]
            d_raw = [mm_nt(both[n], keys) for n in pair]
            weights, d_scores, low_weights, low_d_weights = [], [], [], []
            for n in pair:
                scores = raw[n] * (scale * math.log2(math.e))
                corner = jnp.where(earlier <= position, scores[:, span - ROWS:], -1e30)
                if block:
                    scores = jnp.concatenate([scores[:, :span - ROWS], corner], axis=1)
                else:
                    scores = corner
                top = jnp.max(scores, axis=1, keepdims=True)
                grown = jnp.exp2(scores - top)
                share = grown * (1.0 / jnp.sum(grown, axis=1, keepdims=True))
                moved = d_raw[n] - jnp.sum(share * d_raw[n], axis=1, keepdims=True)
                weights.append(share)
                d_scores.append(moved)
                low_weights.append(share.astype(bf16))
                low_d_weights.append((share * moved).astype(bf16))
            mixed = [mm(low_weights[n], values) for n in pair]
            d_mixed = [mm(low_d_weights[n], values[:, :HD]) for n in pair]
            miss, d_miss, mean, d_mean = [], [], [], []
            for n in pair:
                mixture = mixed[n][:, :HD]
                target = wanted_ref[rows, n * HD:(n + 1) * HD].astype(f32)
                miss.append((mixture - target).astype(bf16))
                d_miss.append((mixed[n][:, HD:] + d_mixed[n] * scale).astype(bf16))
                miss32, d_miss32 = miss[n].astype(f32), d_miss[n].astype(f32)
                mean.append(jnp.sum(miss32 * mixture, axis=1, keepdims=True))
                d_mean.append(
                    jnp.sum(d_miss32 * mixture + miss32 * d_miss32, axis=1, keepdims=True)
                )
            away = [mm_nt(miss[n], values[:, :HD]) for n in pair]
            d_away = [mm_nt(jnp.concatenate([d_miss[n], miss[n]], axis=1), values) for n in pair]
            back, d_back = [], []
            for n in pair:
                off = away[n] - mean[n]
                back.append((weights[n] * off).astype(bf16))
                d_back.append(
                    (weights[n] * (scale * (d_scores[n] * off) + (d_away[n] - d_mean[n]))).astype(bf16)
                )
            for n in pair:
                dual_q = mm(d_back[n], keys[:, :HD]) + mm(back[n], keys[:, HD:])
                low_ref[rows, pl.ds(pl.multiple_of((2 * head + n) * HD, HD), HD)] = unrope(
                    dual_q * (scale * factor), rows
                ).astype(bf16)
            left_k = [part for n in pair for part in (both[n][:, HD:], both[n][:, :HD])]
            right_k = [part for n in pair for part in (d_back[n], back[n])]
            left_v = [
                part for n in pair
                for part in ((miss[n].astype(f32) * scale).astype(bf16), d_miss[n])
            ]
            right_v = [part for n in pair for part in (low_d_weights[n], low_weights[n])]
            dkt[:, :span] += mm(jnp.concatenate(left_k, axis=0).T, jnp.concatenate(right_k, axis=0))
            dvt[:, :span] += mm(jnp.concatenate(left_v, axis=0).T, jnp.concatenate(right_v, axis=0))

    @pl.when((head == members // 2 - 1) & active)
    def _():
        every = pl.ds(0, length)
        low_ref[:, wide:wide + HD] = unrope(dkt[...].T * (scale * factor), every).astype(bf16)
        low_ref[:, wide + HD:] = (dvt[...].T * factor).astype(bf16)


def attention(wanted, first, width, tables, factor, early=None, features=None, slabs=(), places=None):
    length = wanted.shape[0]
    half = width // 2
    members = half // HD - 2
    first = first // (2 * HD)
    late = len(slabs)
    if places is None:
        places = jnp.ones((1,), jnp.int32)
    slow = pl.BlockSpec(memory_space=pltpu.HBM)
    table = pl.BlockSpec((length, HD), lambda h, p: (0, 0))
    early_spec = [slow if late else pl.BlockSpec((length, width), lambda h, p: (0, 0))]
    scratch = [pltpu.VMEM((length, 2 * HD), jnp.bfloat16)] * 2
    scratch += [pltpu.VMEM((2, length, 2 * HD), jnp.bfloat16)]
    scratch += [pltpu.VMEM((HD, length), jnp.float32)] * 2
    if late:
        depth = late * slabs[0].shape[0]
        scratch += [
            pltpu.VMEM((length, width), jnp.float32),
            pltpu.VMEM((length, depth), jnp.bfloat16),
            pltpu.VMEM((depth, width), jnp.bfloat16),
            pltpu.SemaphoreType.DMA((2 * late + 1,)),
        ]
    return pl.pallas_call(
        functools.partial(attention_kernel, members, factor, late, early is not None),
        grid_spec=pltpu.PrefetchScalarGridSpec(
            num_scalar_prefetch=1,
            grid=(members // 2,),
            in_specs=[slow] * (late + 1 if late else 0)
            + (early_spec if early is not None else [])
            + [pl.BlockSpec((length, 2 * HD), lambda h, p: (0, first + h)), table, table],
            out_specs=pl.BlockSpec((length, half), lambda h, p: (0, 0)),
            scratch_shapes=scratch,
        ),
        out_shape=jax.ShapeDtypeStruct((length, half), jnp.bfloat16),
        compiler_params=pltpu.CompilerParams(
            dimension_semantics=("arbitrary",), vmem_limit_bytes=56 * 2 ** 20
        ),
        cost_estimate=SMALL,
        name="attention_curvature",
    )(places, *((features, *slabs) if late else ()), *(() if early is None else (early,)), wanted, *tables)


def pack_kernel(groups, inputs, *refs):
    parts, outs = refs[:inputs], refs[inputs:]
    for g in range(groups):
        left = 0
        for ref in parts:
            width = ref.shape[1] // groups
            outs[g][:, left:left + width] = ref[:, g * width:(g + 1) * width]
            left += width
    if len(refs) > inputs + groups:
        rows, first, second = refs[-3:]
        first[...] = rows[:, :rows.shape[1] // 2]
        second[...] = rows[:, rows.shape[1] // 2:]


def packed(parts, tokens=None):
    rows = parts[0].shape[0]
    groups = parts[1].shape[1] // HD
    shapes = [(rows, sum(part.shape[1] for part in parts) // groups)] * groups
    inputs = list(parts)
    if tokens is not None:
        inputs.append(tokens)
        shapes += [(tokens.shape[0], tokens.shape[1] // 2)] * 2
    steps = 2

    def block(shape):
        return pl.BlockSpec((shape[0] // steps, shape[1]), lambda i: (i, 0))

    def kernel(*refs):
        count = len(inputs)
        if tokens is None:
            return pack_kernel(groups, count, *refs)
        return pack_kernel(groups, count - 1, *refs[:count - 1], *refs[count:count + groups],
                           refs[count - 1], *refs[count + groups:])

    return pl.pallas_call(
        kernel,
        grid=(steps,),
        in_specs=[block(x.shape) for x in inputs],
        out_specs=[block(shape) for shape in shapes],
        out_shape=[jax.ShapeDtypeStruct(shape, parts[0].dtype) for shape in shapes],
        cost_estimate=SMALL,
        name="pack_rows",
    )(*inputs)


def finish_kernel(inner, total_a, home, crossed, back, out_q, out_k, out_v):
    f32 = jnp.float32
    mine = inner[0] == 1
    total_b = jnp.where(
        mine, home[...].astype(f32) + crossed[...].astype(f32), back[...].astype(f32)
    )
    wide = total_b.shape[1] - 2 * HD
    for n, total in enumerate((total_a[...], total_b)):
        out_q[:, n * wide:(n + 1) * wide] = total[:, :wide]
        out_k[:, n * HD:(n + 1) * HD] = total[:, wide:wide + HD]
        out_v[:, n * HD:(n + 1) * HD] = total[:, wide + HD:]


def finish(inner, *terms):
    rows, width = terms[0].shape
    widths = (2 * (width - 2 * HD), 2 * HD, 2 * HD)
    block = rows // 2
    return pl.pallas_call(
        finish_kernel,
        grid_spec=pltpu.PrefetchScalarGridSpec(
            num_scalar_prefetch=1,
            grid=(2,),
            in_specs=[pl.BlockSpec((block, width), lambda i, p: (i, 0))] * len(terms),
            out_specs=[pl.BlockSpec((block, w), lambda i, p: (i, 0)) for w in widths],
        ),
        out_shape=[jax.ShapeDtypeStruct((rows, w), jnp.float32) for w in widths],
        cost_estimate=SMALL,
        name="finish_sums",
    )(inner.astype(jnp.int32)[None], *terms)


def unpacked(sums):
    wide = sums[0].shape[1] - 2 * HD
    return tuple(
        jnp.concatenate([s[:, lo:hi] for s in sums], axis=1)
        for lo, hi in ((0, wide), (wide, wide + HD), (wide + HD, wide + 2 * HD))
    )


def transposed_product(features, low):
    return lax.dot_general(
        features, low, (((0,), (0,)), ((), ())), preferred_element_type=jnp.float32
    ).astype(jnp.bfloat16)


def by_sequence(tokens, target, *parts):
    length = tokens.shape[0]
    factor = (length * lax.axis_size("fsdp")) ** (-0.5)
    groups = parts[1].shape[1] // HD
    wide = target.shape[1] // groups
    features = lax.all_gather(tokens, "tp", axis=1, tiled=True)
    gathered = [lax.all_gather(rows, "fsdp", axis=0, tiled=True) for rows in packed(parts)]
    tables = rope_tables(length, HD)
    sums = []
    for g in range(groups):
        early = mm(features, gathered[g])
        low = attention(target, g * wide, early.shape[1], tables, factor, early)
        part = transposed_product(features, low)
        sums.append(lax.psum_scatter(part, "fsdp", scatter_dimension=0, tiled=True).astype(jnp.float32))
    return unpacked(sums)


def after(value, *others):
    return lax.optimization_barrier((value,) + others)[0]


def inner_heavy(tokens, target, *parts):
    f32, bf16 = jnp.float32, jnp.bfloat16
    length = tokens.shape[0]
    position = lax.axis_index("fsdp")
    chip, core = position // 2, position % 2
    side, low_high = chip // 2, chip % 2
    inner = (chip == 1) | (chip == 2)
    factor = (length * lax.axis_size("fsdp")) ** (-0.5)
    wide = target.shape[1] // 2

    def chips(pairs):
        return [(2 * a + c, 2 * b + c) for a, b in pairs for c in range(2)]

    swap_sides = chips([(0, 1), (1, 0), (2, 3), (3, 2)])
    inwards, outwards = chips([(0, 1), (3, 2)]), chips([(1, 0), (2, 3)])
    middle, beyond = chips([(1, 2), (2, 1)]), chips([(0, 2), (3, 1)])
    middle_out, ends = chips([(1, 3), (2, 0)]), chips([(0, 3), (3, 0)])
    swap_cores = [(n, n ^ 1) for n in range(8)]

    def along(value, pairs):
        return lax.ppermute(value, "fsdp", pairs)

    def other_core(value):
        return along(value, swap_cores)

    def across(value, bit):
        return lax.ppermute(value, "tp", [(n, n ^ bit) for n in range(4)])

    column = lax.axis_index("tp")
    columns = [column ^ bit for bit in (0, 1, 0, 2, 2, 3, 1, 3)]
    oi, oo = jnp.where(side == 0, 2, 1), jnp.where(side == 0, 3, 0)
    hi, ho = 3 - oi, 3 - oo
    slots = [2 * z + c for z in (chip, chip ^ 1, oi, oo) for c in (core, 1 - core)]

    def places(active, which=range(8)):
        return jnp.stack([active] + [slots[n] for n in which]).astype(jnp.int32)

    def plus(*terms):
        return functools.reduce(jnp.add, [term.astype(f32) for term in terms])

    tables = rope_tables(length, HD)

    phase = lax.optimization_barrier
    own_a, own_b, first, second = packed(parts, tokens)
    width = own_a.shape[1]
    x_first, y_second = across(first, 1), across(second, 2)
    side_a, mid_a, own_a2, *tables = phase(
        (along(own_a, swap_sides), along(own_a, middle), other_core(own_a), *tables)
    )
    outer_tokens = along(after(jnp.stack([first, second]), side_a), inwards)
    firsts, seconds = jnp.stack([first, x_first]), jnp.stack([second, y_second])
    pieces = [firsts, seconds, across(firsts, 2), across(seconds, 1)]
    features, mine_t, theirs_t = place(pieces, columns, core)
    late_side, late_mid = phase((side_a, mid_a, features))[:2]
    far_a, out_a, outer_tokens, side_a2, mid_a2, features = phase(
        (
            along(side_a, middle), along(mid_a, outwards), outer_tokens,
            other_core(late_side), other_core(late_mid), features,
        )
    )
    far_a2, out_a2, own_b = other_core(far_a), other_core(out_a), after(own_b, far_a)
    first, second = phase((outer_tokens[0], outer_tokens[1], far_a2, out_a2))[:2]
    def only(flag, call, dtype):
        shape = (length, width // 2 if dtype == bf16 else width)
        return lax.cond(flag, call, lambda: blank(shape, dtype))

    near = [own_a, own_a2, side_a, side_a2]
    inner_low = only(
        inner,
        lambda: attention(
            target, 0, width, tables, factor, None, features,
            near + [mid_a, mid_a2, far_a, far_a2], places(1),
        ),
        bf16,
    )
    early_a = only(
        ~inner, lambda: fold(features, near + [out_a, out_a2], places(1, range(6))), f32
    )
    x_first, y_second, out_far_a, mid_b, side_b, inner_low, early_a = phase(
        (
            across(first, 1), across(second, 2), along(far_a, outwards), along(own_b, middle),
            along(own_b, inwards), inner_low, early_a,
        )
    )
    far_b = along(side_b, middle)
    own_b = after(own_b, inner_low)
    firsts, seconds = jnp.stack([first, x_first]), jnp.stack([second, y_second])
    out_far_a2, side_b2, firsts, seconds = phase(
        (other_core(out_far_a), other_core(side_b), firsts, seconds)
    )
    mid_b, own_b, theirs_t = phase((mid_b, own_b, theirs_t, out_far_a2))[:3]
    pieces = [firsts, seconds, across(firsts, 2), across(seconds, 1)]
    mid_b2 = other_core(mid_b)
    own_b2 = other_core(after(own_b, mid_b2))
    low_a = lax.cond(
        inner,
        lambda: inner_low,
        lambda: attention(
            target, 0, width, tables, factor, early_a, features, [out_far_a, out_far_a2],
            places(1, (6, 7)),
        ),
    )
    rows_t, lows = [mine_t, other_core(theirs_t)], [low_a, other_core(low_a)]

    slabs_b = [own_b, own_b2, side_b, side_b2, mid_b, mid_b2]
    early = fold(after(features, low_a), slabs_b, places(inner, range(6)))
    sums = gradient(rows_t, lows, after(jnp.stack([oo, oi, ho, hi]), early), 4)
    far_b, early, sums, pieces = phase((far_b, early, [part[0] for part in sums], pieces))
    away, home = sums[:2], sums[2:]
    far_b2 = other_core(far_b)
    from_inner = along(away[1], middle), along(away[0], middle_out)
    home_swap = along(jnp.where(inner, home[0], home[1]), swap_sides)
    outer_wanted = along(after(target[:, wide:], far_b), inwards)
    own_low = attention(
        target, wide, width, tables, factor, early, features, [far_b, far_b2],
        places(inner, (6, 7)),
    )
    pieces[0] = after(pieces[0], own_low)
    outer_features, mine_t, theirs_t = place(pieces, columns, core)
    from_inner, home_swap, outer_wanted, own_low, outer_features, theirs_t = phase(
        (from_inner, home_swap, outer_wanted, own_low, outer_features, theirs_t)
    )
    away = phase((away, from_inner))[0]
    from_outer = along(away[1], beyond), along(away[0], ends)
    own_low2, theirs_t = other_core(own_low), other_core(theirs_t)
    outer_low = attention(
        outer_wanted, 0, width, tables, factor, None, outer_features,
        slabs_b + [far_b, far_b2], places(inner),
    )
    rows_t += [mine_t, theirs_t]
    lows = [own_low, own_low2, outer_low, other_core(after(outer_low, *from_outer))]
    ready = phase((jnp.stack([oo, oi, ho, hi]), theirs_t, own_low2))[0]
    away_out = gradient(rows_t, lows, ready[:1])[0][0]
    home_out = gradient(rows_t, lows, after(ready[2:3], away_out))[0][0]
    lows[0] = after(lows[0], home_out)
    away_in = gradient(rows_t, lows, ready[1:2])[0][0]
    lows[0] = after(lows[0], away_in)
    home_in = gradient(rows_t, lows, ready[3:])[0][0]
    crossed_out, crossed_in = along(away_out, middle), along(away_in, middle)
    total_a = jnp.where(inner, home[1], home[0]).astype(f32) + plus(
        home_swap, *from_inner, *from_outer
    )
    back_b = along(plus(home_out, crossed_out).astype(bf16), outwards)
    return finish(inner, total_a, home_in, crossed_in, back_b)


def solution(mesh):
    spec = P("fsdp", "tp")

    def shards(*args):
        groups = args[3].shape[1] // HD
        if mesh.shape["fsdp"] == 8 and mesh.shape["tp"] == 4 and groups == 2:
            return tuple(inner_heavy(*args))
        return by_sequence(*args)

    return jax.shard_map(
        shards,
        mesh=mesh,
        in_specs=(spec,) * 8,
        out_specs=(spec,) * 3,
        check_vma=False,
    )
```
